512 devices in a mesh: group: 32 (over x, y, core), tile: 16 (over z).
Axes of the slice: x: 4, y: 4, z: 16, core: 2. Of those that a mesh axis runs over, the one named last changes fastest.
Arguments:
- block_input_frames: bfloat16 [32, 4, 16, 4, 8, 512], P('group', None, 'tile'), may hold values from -6 to 6
- norm_gain: float32 [512], replicated, may hold values from 0.25 to 1.75
- kernel: bfloat16 [3, 3, 3, 512, 512], P(None, None, None, 'group', 'tile'), may hold values from -0.0546875 to 0.0546875
- output_gradient: bfloat16 [32, 4, 16, 4, 8, 512], P('group', None, 'tile'), may hold values from -6 to 6
- group_count: int32 [32], P('group'), may hold values from 1 to 1, as said below
- clip_starts: int32 [32], P('group'), may hold values 0 or 1
Outputs:
- block_out: bfloat16 [32, 4, 16, 4, 8, 512], P('group', None, 'tile')
- input_grad: bfloat16 [32, 4, 16, 4, 8, 512], P('group', None, 'tile')
The draws below stay inside these ranges and needn't reach their ends.
Inputs may be any that keep to these rules, and one draw needn't show every extreme that they name: `group_count`: each entry lies in 1 to 1, and some index of group holds 1 group.
All inputs are finite; a program needn't handle non-finite values. No bound on the sum of `clip_starts` on one device may be relied on, other than what follows from the above.
Results may differ from the reference program's by a relative error of at most 0.0045.
Values may be sent and summed in bfloat16 or wider, within the bound.
A program may use at most 64 MiB of HBM per device.

```python
import jax
import jax.numpy as jnp
from jax import lax

CHANNEL_COUNT = 512
GROUP_FRAMES = 4
SLOTS = 1
TILE_HEIGHT = 4
TILE_WIDTH = 8
SLOT_TOTAL = 32
TCOLS = 4
N_GROUP = 32
N_TILE = 16


def draw_group_count(key, part):
    key = jax.random.fold_in(key, 11)
    first_key, second_key = jax.random.split(key)
    counts = jax.random.randint(first_key, (N_GROUP,), 1, SLOTS + 1)
    full_at = jax.random.randint(second_key, (), 0, N_GROUP)
    positions = jnp.arange(N_GROUP, dtype=jnp.int32)
    return jnp.where(positions == full_at, SLOTS, counts).astype(jnp.int32)


def place_ends(entries, own_key, smallest, top_value):
    shape = entries.shape
    place = [jax.random.randint(jax.random.fold_in(own_key, axis), (), 0, shape[axis]) for axis in range(len(shape))]
    entries = entries.at[tuple(place)].set(smallest)
    longest = shape.index(max(shape))
    place[longest] = (place[longest] + 1) % shape[longest]
    return entries.at[tuple(place)].set(top_value)


def levels(rng, extent, shards, least, largest):
    level = 1.0
    for position, shards_of in shards:
        draws = jax.random.uniform(jax.random.fold_in(jax.random.fold_in(rng, 6), position), (shards_of,), jnp.float32, least / len(shards), largest / len(shards))
        level = level * jnp.repeat(jnp.exp(draws), extent[position] // shards_of).reshape((-1,) + (1,) * (len(extent) - 1 - position))
    return level


def normal_values(rng, extent, scale, reach, shards=(), kind=jnp.bfloat16):
    level = levels(rng, extent, shards, -0.22, 0.18) if shards else 1.0
    values = jax.random.normal(rng, extent, jnp.float32) * scale * level
    return jnp.minimum(jnp.maximum(values, -reach), reach).astype(kind)


def setup_inputs(seed: int = 0) -> dict:
    seeds = jax.random.split(jax.random.key(seed), 7)
    block_input_frames = normal_values(seeds[0], (SLOT_TOTAL, GROUP_FRAMES, N_TILE, TILE_HEIGHT, TILE_WIDTH, CHANNEL_COUNT), 1.0, 6.0, ((0, 32), (2, 16)))
    norm_gain = jnp.clip(1.0 + 0.15 * jax.random.normal(seeds[1], (CHANNEL_COUNT,), jnp.float32), 0.25, 1.75)
    kernel = normal_values(seeds[2], (3, 3, 3, CHANNEL_COUNT, CHANNEL_COUNT), (27 * CHANNEL_COUNT) ** -0.5, 0.0546875, ((3, 32), (4, 16)))
    output_gradient = normal_values(seeds[3], (SLOT_TOTAL, GROUP_FRAMES, N_TILE, TILE_HEIGHT, TILE_WIDTH, CHANNEL_COUNT), 1.0, 6.0, ((0, 32), (2, 16)))
    group_count = draw_group_count(jax.random.fold_in(seeds[6], 71), 0)
    clip_starts = place_ends((jax.random.randint(seeds[5], (SLOT_TOTAL,), 0, 4) < 1).astype(jnp.int32), jax.random.fold_in(seeds[5], 1), 0, 1)
    return {"block_input_frames": block_input_frames, "norm_gain": norm_gain, "kernel": kernel, "output_gradient": output_gradient, "group_count": group_count, "clip_starts": clip_starts}


epsilon = 1e-06

def to_image(field):
    slot_count, frame_count = (field.shape[0], field.shape[1])
    field = field.reshape(slot_count, frame_count, N_TILE // TCOLS, TCOLS, TILE_HEIGHT, TILE_WIDTH, CHANNEL_COUNT)
    field = field.transpose(0, 1, 2, 4, 3, 5, 6)
    return field.reshape(slot_count, frame_count, N_TILE // TCOLS * TILE_HEIGHT, TCOLS * TILE_WIDTH, CHANNEL_COUNT)

def from_image(field):
    slot_count, frame_count = (field.shape[0], field.shape[1])
    field = field.reshape(slot_count, frame_count, N_TILE // TCOLS, TILE_HEIGHT, TCOLS, TILE_WIDTH, CHANNEL_COUNT)
    field = field.transpose(0, 1, 2, 4, 3, 5, 6)
    return field.reshape(slot_count, frame_count, N_TILE, TILE_HEIGHT, TILE_WIDTH, CHANNEL_COUNT)

def conv_taps(padded, kernel, frame_count, height, width, backward):
    channels = padded.shape[4]
    accumulated = jnp.zeros((padded.shape[0] * frame_count * height * width, channels), jnp.float32)
    for step_t in range(3):
        for step_i in range(3):
            for step_j in range(3):
                window_view = padded[:, step_t:step_t + frame_count, step_i:step_i + height, step_j:step_j + width, :]
                window_view = window_view.reshape(-1, channels)
                if backward:
                    kernel_tap = kernel[2 - step_t, 2 - step_i, 2 - step_j].T
                else:
                    kernel_tap = kernel[step_t, step_i, step_j]
                accumulated = accumulated + jnp.dot(window_view, kernel_tap, preferred_element_type=jnp.float32)
    return accumulated.reshape(padded.shape[0], frame_count, height, width, channels)

def normalize(field, gain):
    values = field.astype(jnp.float32)
    scale = lax.rsqrt(lax.optimization_barrier(jnp.mean(values * values, axis=-1, keepdims=True)) + epsilon)
    normed = values * scale * gain.astype(jnp.float32)
    return (values, scale, normed)

def norm_grad(values, scale, normed, gain, upstream):
    sigma = jax.nn.sigmoid(normed)
    through = upstream * sigma * (1.0 + normed * (1.0 - sigma)) * gain.astype(jnp.float32)
    cubed = scale * scale * scale
    return scale * through - values * cubed * lax.optimization_barrier(jnp.mean(values * through, axis=-1, keepdims=True))

def reference(block_input_frames, norm_gain, kernel, output_gradient, group_count, clip_starts):
    slot_indices = jnp.arange(SLOT_TOTAL, dtype=jnp.int32)
    owner = slot_indices // SLOTS
    within = slot_indices % SLOTS
    live_mask = within < group_count[owner]
    previous_count = group_count[jnp.maximum(owner - 1, 0)]
    sender_slot = jnp.where(within > 0, slot_indices - 1, (owner - 1) * SLOTS + previous_count - 1)
    sender_slot = jnp.clip(sender_slot, 0, SLOT_TOTAL - 1).astype(jnp.int32)
    has_source = live_mask & (clip_starts == 0) & (slot_indices > 0)
    source_wide = has_source[:, None, None, None, None]
    live_wide = live_mask[:, None, None, None, None]
    image = to_image(block_input_frames)
    height, width = (image.shape[2], image.shape[3])
    values, scale, normed = normalize(image, norm_gain)
    activated = (normed * jax.nn.sigmoid(normed)).astype(jnp.bfloat16)
    tails = activated[:, GROUP_FRAMES - 2:]
    cache = jnp.where(source_wide, tails[sender_slot], jnp.zeros_like(tails))
    extended = jnp.concatenate([cache, activated], axis=1)
    padded = jnp.pad(extended, ((0, 0), (0, 0), (1, 1), (1, 1), (0, 0)))
    mixed = conv_taps(padded, kernel, GROUP_FRAMES, height, width, False)
    block_out = jnp.where(live_wide, values + mixed, jnp.float32(0.0)).astype(jnp.bfloat16)
    masked_grad = jnp.where(live_wide, to_image(output_gradient), jnp.zeros_like(image))
    grad_padded = jnp.pad(masked_grad, ((0, 0), (2, 2), (1, 1), (1, 1), (0, 0)))
    spread = conv_taps(grad_padded, kernel, GROUP_FRAMES + 2, height, width, True)
    heads = jnp.where(source_wide, spread[:, :2], jnp.float32(0.0))
    tail_grad = jnp.zeros_like(heads).at[sender_slot].add(heads)
    upstream = jnp.concatenate([spread[:, 2:GROUP_FRAMES], spread[:, GROUP_FRAMES:] + tail_grad], axis=1)
    gradient = masked_grad.astype(jnp.float32) + norm_grad(values, scale, normed, norm_gain, upstream)
    input_grad = jnp.where(live_wide, gradient, jnp.float32(0.0)).astype(jnp.bfloat16)
    return (from_image(block_out), from_image(input_grad))
```

```python
import numpy as np
import jax
import jax.numpy as jnp
from jax import lax
from jax.experimental import pallas as pl
from jax.experimental.pallas import tpu as pltpu
from jax.sharding import PartitionSpec as P

MESH = pl.DeviceIdType.MESH
EPSILON = 1e-06
F32, BF16 = jnp.float32, jnp.bfloat16


def swap_table():
    table = np.zeros((512, 512), np.float32)
    for a in range(4):
        for b in range(4):
            for o in range(32):
                table[a * 128 + b * 32 + o, b * 128 + a * 32 + o] = 1
    return table.reshape(512, 4, 128).transpose(1, 0, 2)


def column_table():
    table = np.zeros((32, 128), np.float32)
    for it in range(16):
        table[it, it * 8 + 7] = 1
        table[16 + it, it * 8] = 1
    return table


def corner_table():
    table = np.zeros((4, 64, 128), np.float32)
    for k in range(4):
        for corner, (i, j) in enumerate(((3, 7), (3, 0), (0, 7), (0, 0))):
            for t in range(4):
                table[k, 16 * corner + 4 * k + t, (i * 4 + t) * 8 + j] = 1
    return table


def edge_table():
    table = np.zeros((4, 64, 128), np.float32)
    for k in range(4):
        for side in range(2):
            for t in range(4):
                first = 16 * t + 8 * side
                table[k, first, 32 + 16 * side + 4 * k + t] = 1
                table[k, first + 5, 64 + 16 * side + 4 * k + t] = 1
                for i in range(4):
                    table[k, first + 1 + i, 16 * side + i * 4 + t] = 1
    return table


SHARDS = (0, -1, 7, -4, -7, 4, 1, -2, 6, -5, -8, 3, -3, -6, 5, 2)
CHUNKS = ((0, 1, 0), (1, 3, 0), (4, 3, 1), (7, 5, 0), (12, 4, 1))
STRIP_STEPS, COLUMN_STEPS, CORNER_STEPS = (4, -4), (1, -1), (5, 3, -3, -5)


def dot(left, right):
    return jnp.dot(left, right, preferred_element_type=F32)


def swap_lanes(value, swap_ref):
    return dot(value, jnp.concatenate([swap_ref[k] for k in range(4)], axis=1))


def body(
    x_hbm, gain_hbm, w_hbm, g_hbm, count_ref, starts_ref, swap_hbm, column_hbm, corner_hbm, edge_hbm,
    out_ref, grad_ref,
    xv, gainv, wv, gv, swap_ref, column_pick, corner_pick, edge_pick,
    wz, wbuf, tsend, trecv, rows_s, rows_r, corners_s, corners_r, amsg, abuf, gb, fbuf, bbuf,
    acc_f, acc_b, psend, precv, bsend, brecv, dsend, drecv, mix,
    in_s, z_s, z_r, t_s, t_r, h_s, h_r, a_s, a_r, gy_s, gy_r,
    wx_s, wx_r, wf_s, wf_r, wc_s, wc_r, p_s, p_r, b_s, b_r, d_s, d_r,
):
    loads = [
        pltpu.make_async_copy(src, dst, in_s.at[k])
        for k, (src, dst) in enumerate(
            (
                (w_hbm, wv), (g_hbm, gv), (x_hbm, xv), (gain_hbm, gainv), (swap_hbm, swap_ref),
                (column_hbm, column_pick), (corner_hbm, corner_pick), (edge_hbm, edge_pick),
            )
        )
    ]
    for load in loads:
        load.start()

    group = lax.axis_index("group")
    z = lax.axis_index("tile")
    x, y, c = lax.div(group, 8), lax.rem(lax.div(group, 2), 4), lax.rem(group, 2)

    def device(x_at, y_at, c_at, z_at):
        return (x_at * 8 + y_at * 2 + c_at, z_at)

    def mod4(value):
        return lax.rem(value + 4, 4)

    def zmove(step):
        return (group, lax.rem(z + step + 16, 16))

    core = device(x, y, 1 - c, z)
    x_right, x_left = device(mod4(x + 1), y, c, z), device(mod4(x - 1), y, c, z)
    y_peers = [device(x, mod4(y + d), c, z) for d in (1, 2, 3)]
    y_right, y_left = y_peers[0], y_peers[2]
    following, previous = lax.rem(group + 1, 32), lax.rem(group + 31, 32)
    after, before = (following, z), (previous, z)
    head_targets = [(lax.rem(x * 8 + 2 * k + c + 31, 32), z) for k in range(4)]
    head_sources = [device(lax.div(following, 8), k, lax.rem(following, 2), z) for k in range(4)]

    barrier = pltpu.get_barrier_semaphore()
    partners = [core, x_right, x_left, *y_peers, after, before, *head_sources]
    partners += [zmove(step) for step in STRIP_STEPS + COLUMN_STEPS + CORNER_STEPS + (7, -7)]
    for partner in partners:
        pl.semaphore_signal(barrier, inc=1, device_id=partner, device_id_type=MESH)

    started = []

    def remote(src, dst, send_sem, recv_sem, target):
        return pltpu.make_async_remote_copy(
            src_ref=src, dst_ref=dst, send_sem=send_sem, recv_sem=recv_sem, device_id=target, device_id_type=MESH
        )

    def send(src, dst, send_sem, recv_sem, target):
        copy = remote(src, dst, send_sem, recv_sem, target)
        copy.start()
        started.append(copy)

    def arrived(dst, sem):
        remote(dst, dst, sem, sem, core).wait_recv()

    def z_first():
        for k, step in enumerate(SHARDS[1:7]):
            send(wz.at[x, 0], wz.at[x, 1 + k], z_s.at[k], z_r.at[k], zmove(-step))

    def z_first_wait():
        for k in range(6):
            arrived(wz.at[x, 1 + k], z_r.at[k])

    def z_second():
        send(wz.at[x, pl.ds(1, 5)], wz.at[x, pl.ds(7, 5)], z_s.at[6], z_r.at[6], zmove(1))
        send(wz.at[x, pl.ds(3, 4)], wz.at[x, pl.ds(12, 4)], z_s.at[7], z_r.at[7], zmove(-1))

    def z_second_wait():
        arrived(wz.at[x, pl.ds(7, 5)], z_r.at[6])
        arrived(wz.at[x, pl.ds(12, 4)], z_r.at[7])

    def x_block(step, k):
        return wz.at[mod4(x + step), pl.ds(CHUNKS[k][0], CHUNKS[k][1])]

    def x_send(k, side):
        block = x_block(0, k)
        send(block, block, wx_s.at[side, k], wx_r.at[side, k], x_left if side else x_right)

    def x_arrived(k, side):
        arrived(x_block(1 if side else -1, k), wx_r.at[side, k])

    def x_pass(k):
        side = CHUNKS[k][2]
        x_arrived(k, side)
        block = x_block(1 if side else -1, k)
        send(block, block, wf_s.at[k], wf_r.at[k], x_left if side else x_right)

    def x_far(k):
        arrived(x_block(2, k), wf_r.at[k])

    places = []
    for shard in range(16):
        away = lax.rem(shard - z + 24, 16) - 8
        place = jnp.int32(0)
        for slot in range(1, 16):
            place = jnp.where(away == SHARDS[slot], slot, place)
        places.append(place)

    def w_layout(step):
        at = mod4(x + step)
        rows = []
        for quad in range(4):
            rows.append(jnp.concatenate([wz[at, places[quad * 4 + j]] for j in range(4)], axis=1))
        full = swap_lanes(jnp.concatenate(rows, axis=0), swap_ref).astype(BF16)
        for quad in range(4):
            for tap in range(27):
                row, lanes = quad * 112 + (tap // 4) * 16, (tap % 4) * 128
                wbuf[c, at, quad, tap] = full[row : row + 16, lanes : lanes + 128]
        whole = wbuf.at[c, at]
        send(whole, whole, wc_s.at[step + 1], wc_r.at[step + 1], core)

    def w_core():
        for step in (0, -1, 1, 2):
            arrived(wbuf.at[1 - c, mod4(x + step)], wc_r.at[step + 1])

    def y_block(owner, half, part):
        return gb.at[owner, pl.ds(2 * half, 2), pl.ds(128 * part, 128)]

    def y_start(part):
        for half in range(2):
            block = y_block(y, half, part)
            send(block, block, gy_s.at[part, 0, half], gy_r.at[part, 0, half], y_right)
            send(block, block, gy_s.at[part, 1, half], gy_r.at[part, 1, half], y_left)

    def y_relay(part):
        for side, step, target in ((0, -1, y_right), (1, 1, y_left)):
            for half in (side, 1 - side):
                block = y_block(mod4(y + step), half, part)
                arrived(block, gy_r.at[part, side, half])
                if half == side:
                    send(block, block, gy_s.at[part, 2, half], gy_r.at[part, 2, half], target)

    def y_far(part):
        for half in range(2):
            arrived(y_block(mod4(y + 2), half, part), gy_r.at[part, 2, half])

    def strips_start(field, tile):
        rows_s[field, 0:32] = tile[96:128]
        rows_s[field, 32:64] = tile[0:32]
        for k, step in enumerate(STRIP_STEPS):
            block = pl.ds(32 * k, 32)
            send(rows_s.at[field, block], rows_r.at[field, block], h_s.at[field, k], h_r.at[field, k], zmove(step))

    def columns_start(field, tile):
        rows_s[field, 64:96] = dot(column_pick[...], tile).astype(BF16)
        for k, step in enumerate(COLUMN_STEPS):
            block = pl.ds(64 + 16 * k, 16)
            send(rows_s.at[field, block], rows_r.at[field, block], h_s.at[field, 2 + k], h_r.at[field, 2 + k], zmove(step))
        corners = [dot(corner_pick[k], tile[:, k * 128 : (k + 1) * 128]) for k in range(4)]
        corners_s[field] = (corners[0] + corners[1] + corners[2] + corners[3]).astype(BF16)
        for k, step in enumerate(CORNER_STEPS):
            block = pl.ds(16 * k, 16)
            send(corners_s.at[field, block], corners_r.at[field, block], h_s.at[field, 4 + k], h_r.at[field, 4 + k], zmove(step))

    tile_row, tile_column = lax.div(z, 4), lax.rem(z, 4)

    def unless(hit):
        return jnp.where(hit, 0.0, 1.0).astype(F32)

    at_top, at_bottom = unless(tile_row == 0), unless(tile_row == 3)
    at_left, at_right = unless(tile_column == 0), unless(tile_column == 3)

    def halo_finish(field):
        for k in range(2):
            arrived(rows_r.at[field, pl.ds(32 * k, 32)], h_r.at[field, k])
        for k in range(2):
            arrived(rows_r.at[field, pl.ds(64 + 16 * k, 16)], h_r.at[field, 2 + k])
        for k in range(4):
            arrived(corners_r.at[field, pl.ds(16 * k, 16)], h_r.at[field, 4 + k])
        above = rows_r[field, 0:32].astype(F32) * at_top
        below = rows_r[field, 32:64].astype(F32) * at_bottom
        row_at = lax.broadcasted_iota(jnp.int32, (64, 128), 0)
        keep = jnp.where((row_at & 8) == 0, at_left, at_right)
        keep = keep * jnp.where((row_at & 7) == 0, at_top, 1.0) * jnp.where((row_at & 7) == 5, at_bottom, 1.0)
        flag = jnp.where(row_at == 6, source, 0.0)
        edges = []
        for k in range(4):
            picks = jnp.concatenate([rows_r[field, 64:96, k * 128 : (k + 1) * 128], corners_r[field]], axis=0)
            edges.append(dot(edge_pick[k, :, 0:96], picks) * keep + flag)
        return jnp.concatenate([above, below, jnp.concatenate(edges, axis=1)], axis=0).astype(BF16)

    loads[0].wait()
    packed = jnp.zeros((112, 128), F32)
    for k in range(4):
        taps = [wv[4 * row + k] if 4 * row + k < 27 else jnp.zeros((16, 32), BF16) for row in range(7)]
        lane_at = lax.broadcasted_iota(jnp.int32, (32, 128), 1) - lax.broadcasted_iota(jnp.int32, (32, 128), 0)
        packed = packed + dot(jnp.concatenate(taps, axis=0), jnp.where(lane_at == 32 * k, 1.0, 0.0).astype(BF16))
    wz[x, 0] = packed.astype(BF16)

    live = jnp.where(count_ref[0] > 0, 1.0, 0.0).astype(F32)
    fresh = jnp.where(starts_ref[0] == 0, 1.0, 0.0).astype(F32)
    source = live * fresh * jnp.where(group > 0, 1.0, 0.0).astype(F32)

    def swap_frames(value):
        value = value.reshape(4, 4, 8, value.shape[1])
        return jnp.concatenate([value[:, k] for k in range(4)], axis=0).reshape(128, value.shape[3])

    loads[1].wait()
    masked = gv[...].astype(F32) * live
    grad_tile = swap_frames(masked).astype(BF16)
    for k in range(4):
        gb[y, k, 0:128] = grad_tile[:, k * 128 : (k + 1) * 128]

    pl.semaphore_wait(barrier, len(partners))
    z_first()
    x_send(0, 0)
    x_send(0, 1)
    y_start(0)

    loads[2].wait()
    loads[3].wait()
    loads[4].wait()
    gain = gainv[...]
    values = xv[...].astype(F32)
    scale = lax.rsqrt(jnp.mean(values * values, axis=-1, keepdims=True) + EPSILON)
    normed = values * scale * gain
    activated = (normed * jax.nn.sigmoid(normed)).astype(BF16)
    swapped = swap_lanes(activated, swap_ref)
    tsend[0:64] = swapped[64:128].astype(BF16)
    act_tile = swap_frames(swapped).astype(BF16)

    def a_rows(part):
        return pl.ds(0, 128) if part == 0 else pl.ds(128, 256)

    def a_start(part, value):
        first = 0 if part == 0 else 128
        for k in range(4):
            amsg[k, first : first + value.shape[0]] = value[:, k * 128 : (k + 1) * 128]
        for d in (1, 2, 3):
            src, dst = amsg.at[mod4(y + d), a_rows(part)], abuf.at[y, a_rows(part)]
            send(src, dst, a_s.at[part, d - 1], a_r.at[part, d - 1], y_peers[d - 1])
        abuf[y, first : first + value.shape[0]] = amsg[y, first : first + value.shape[0]]

    def a_wait(part):
        for d in (1, 2, 3):
            arrived(abuf.at[mod4(y - d), a_rows(part)], a_r.at[part, d - 1])

    a_start(0, act_tile)
    for load in loads[5:]:
        load.wait()
    strips_start(0, act_tile)
    columns_start(0, act_tile)
    z_first_wait()
    z_second()
    for k, side in ((1, 0), (2, 1), (2, 0), (1, 1)):
        x_send(k, side)
    x_pass(0)
    strips_start(1, grad_tile)
    columns_start(1, grad_tile)
    y_relay(0)
    halo = halo_finish(0)
    tsend[64:80] = halo[16:32]
    tsend[80:96] = halo[48:64]
    tsend[96:128] = halo[96:128]
    send(tsend, trecv, t_s.at[0], t_r.at[0], after)
    z_second_wait()
    for k, side in ((3, 0), (4, 1), (4, 0), (3, 1)):
        x_send(k, side)
    x_pass(1)
    x_pass(2)
    w_layout(0)
    arrived(trecv, t_r.at[0])
    a_start(1, jnp.concatenate([halo, (trecv[...].astype(F32) * source).astype(BF16)], axis=0))
    grad_halo = halo_finish(1)
    for k in range(4):
        gb[y, k, 128:256] = grad_halo[:, k * 128 : (k + 1) * 128]
    y_start(1)
    x_pass(3)
    x_pass(4)
    for k in range(5):
        x_arrived(k, 1 - CHUNKS[k][2])
    w_layout(-1)
    w_layout(1)
    y_relay(1)

    def shifted(slabs, centers, edges):
        center = jnp.concatenate([slabs[k : k + 1] for k in centers], axis=0)
        sides = []
        for side in range(2):
            rows = [jnp.broadcast_to(slabs[k + side, i : i + 1], slabs.shape[1:])[None] for k, i in edges]
            sides.append(jnp.concatenate(rows, axis=0))
        at = lax.broadcasted_iota(jnp.int32, center.shape, 1)
        from_left = jnp.where(at == 0, sides[0], pltpu.roll(center, 1, 1))
        from_right = jnp.where(at == 7, sides[1], pltpu.roll(center, 7, 1))
        return from_left, center, from_right

    def own_slab(i, t):
        return 16 + t if i == 0 else 20 + t if i == 5 else (i - 1) * 4 + t

    def carried_slab(i, t):
        return 40 + t if i == 0 else 42 + t if i == 5 else 32 + t * 4 + i - 1

    grad_centers = [own_slab(i, t) for i in range(6) for t in range(4)]
    grad_edges = [(24 + 2 * t, i) for i in range(6) for t in range(4)]
    act_centers = [carried_slab(i, t) if t < 2 else own_slab(i, t - 2) for i in range(6) for t in range(6)]
    act_edges = [(44 + 2 * t, i) if t < 2 else (24 + 2 * (t - 2), i) for i in range(6) for t in range(6)]

    a_wait(0)
    a_wait(1)

    def build_f(pair, carry):
        parts = []
        for k in range(2):
            slabs = abuf[2 * pair + k].astype(F32).reshape(48, 8, 128)
            parts.append(shifted(slabs, act_centers, act_edges))
        rows = pl.ds(pl.multiple_of(16 * pair, 16), 16)
        for e in range(3):
            value = jnp.concatenate([part[e] for part in parts], axis=1).astype(BF16)
            fbuf[e, :, :, rows] = value.reshape(6, 6, 16, 128)
        return carry

    lax.fori_loop(0, 2, build_f, 0)
    for k in range(5):
        x_far(k)
    w_layout(2)

    def build_g(k, carry):
        half, pair = lax.div(k, 2), lax.rem(k, 2)
        parts = []
        for n in range(2):
            message = jnp.concatenate([gb[2 * pair + n, 2 * half + m] for m in range(2)], axis=1)
            parts.append(shifted(message.astype(F32).reshape(32, 8, 256), grad_centers, grad_edges))
        rows = pl.ds(pl.multiple_of(16 * pair, 16), 16)
        for e in range(3):
            value = jnp.concatenate([part[e] for part in parts], axis=1).astype(BF16)
            for m in range(2):
                bbuf[2 * half + m, e, :, :, rows] = value[:, :, m * 128 : (m + 1) * 128].reshape(6, 4, 16, 128)
        return carry

    def taps_of(r, tap):
        return jnp.concatenate([wbuf[k, i, r, tap] for i in range(4) for k in range(2)], axis=0)

    def forward(pair):
        acc_f[...] = jnp.zeros_like(acc_f)

        def frame_tap(a, carry):
            windows, taps = [], []
            for b in range(3):
                for e in range(3):
                    windows.append(fbuf[e, b : b + 4, pl.ds(a, 4)].reshape(512, 128))
                    tap = a * 9 + b * 3 + e
                    taps.append(jnp.concatenate([taps_of(2 * pair + k, tap) for k in range(2)], axis=1))
            acc_f[...] += dot(jnp.concatenate(windows, axis=1), jnp.concatenate(taps, axis=0))
            return carry

        lax.fori_loop(0, 3, frame_tap, 0)
        total = acc_f[...].reshape(16, 32, 256)
        for other in range(4):
            psend[pair, other] = total[:, other * 8 : other * 8 + 8].reshape(128, 256).astype(BF16)
        for d in (1, 2, 3):
            send(psend.at[pair, mod4(y + d)], precv.at[pair, d - 1], p_s.at[pair, d - 1], p_r.at[pair, d - 1], y_peers[d - 1])

    def backward(pair):
        def row_tap(b, carry):
            windows, taps = [], []
            for e in range(3):
                for r in (2 * pair, 2 * pair + 1):
                    windows.append(bbuf[r, 2 - e, pl.ds(2 - b, 4)].reshape(512, 128))
                    taps.append(jnp.concatenate([taps_of(r, a * 9 + b * 3 + e) for a in range(3)], axis=0))
            acc_b[...] += lax.dot_general(
                jnp.concatenate(windows, axis=1),
                jnp.concatenate(taps, axis=1),
                (((1,), (1,)), ((), ())),
                preferred_element_type=F32,
            )
            return carry

        lax.fori_loop(0, 3, row_tap, 0)

    def reduce(pair):
        total = psend[pair, y].astype(F32)
        for d in (1, 2, 3):
            arrived(precv.at[pair, d - 1], p_r.at[pair, d - 1])
            total = total + precv[pair, d - 1].astype(F32)
        mix[2 * pair] = total[:, 0:128]
        mix[2 * pair + 1] = total[:, 128:256]

    y_far(0)
    y_far(1)
    lax.fori_loop(0, 4, build_g, 0)
    acc_b[...] = jnp.zeros_like(acc_b)
    w_core()
    forward(0)
    forward(1)
    backward(0)
    backward(1)
    taps = acc_b[...].reshape(4, 4, 32, 384)
    spread = []
    for u in range(6):
        terms = [taps[:, u - a, :, a * 128 : (a + 1) * 128] for a in range(3) if 0 <= u - a < 4]
        spread.append(sum(terms[1:], terms[0]))
    for other in range(4):
        slots = [part[:, other * 8 : other * 8 + 8] for part in spread]
        bsend[other] = jnp.stack(slots[2:], axis=1).reshape(128, 128).astype(BF16)
        flag = gb[other, 0, 192:208].astype(F32)[6:7]
        dsend[other] = (jnp.stack(slots[:2], axis=1).reshape(64, 128) * flag).astype(BF16)
    for d in (1, 2, 3):
        send(bsend.at[mod4(y + d)], brecv.at[y], b_s.at[d - 1], b_r.at[d - 1], y_peers[d - 1])
    for k in range(4):
        send(dsend.at[k], drecv.at[y], d_s.at[k], d_r.at[y], head_targets[k])
    brecv[y] = bsend[y]
    reduce(0)
    reduce(1)
    mixed = jnp.concatenate([mix[k] for k in range(4)], axis=1)
    out_ref[...] = ((values + swap_frames(mixed)) * live).astype(BF16)
    for copy in started[:-7]:
        copy.wait_send()
    for d in (1, 2, 3):
        arrived(brecv.at[mod4(y - d)], b_r.at[d - 1])
    for k in range(4):
        arrived(drecv.at[k], d_r.at[k])
    own = jnp.concatenate([brecv[k] for k in range(4)], axis=1).astype(F32).reshape(4, 4, 8, 512)
    heads = jnp.concatenate([drecv[k] for k in range(4)], axis=1).astype(F32).reshape(4, 2, 8, 512)
    upstream = swap_lanes(own.reshape(128, 512).astype(BF16), swap_ref).reshape(4, 4, 8, 512)
    tails = swap_lanes(heads.reshape(64, 512).astype(BF16), swap_ref).reshape(4, 2, 8, 512)
    upstream = jnp.concatenate(
        [upstream[:, 0], upstream[:, 1], upstream[:, 2] + tails[:, 0], upstream[:, 3] + tails[:, 1]], axis=0
    ).reshape(128, 512)
    sigma = jax.nn.sigmoid(normed)
    through = upstream * sigma * (1.0 + normed * (1.0 - sigma)) * gain
    cubed = scale * scale * scale
    through_mean = jnp.mean(values * through, axis=-1, keepdims=True)
    gradient = masked + scale * through - values * cubed * through_mean
    grad_ref[...] = (gradient * live).astype(BF16)
    for copy in started[-7:]:
        copy.wait_send()


def pin(value):
    return pltpu.with_memory_space_constraint(value, pltpu.HBM)


def per_device(block_input_frames, norm_gain, kernel, output_gradient, group_count, clip_starts):
    shape = block_input_frames.shape
    tables = [jnp.asarray(table(), BF16) for table in (swap_table, column_table, corner_table, edge_table)]
    vmem, smem, hbm = [pl.BlockSpec(memory_space=space) for space in (pltpu.VMEM, pltpu.SMEM, pltpu.HBM)]
    dma = pltpu.SemaphoreType.DMA
    block_out, input_grad = pl.pallas_call(
        body,
        out_shape=[jax.ShapeDtypeStruct((128, 512), BF16)] * 2,
        in_specs=[hbm] * 4 + [smem] * 2 + [hbm] * 4,
        out_specs=[vmem] * 2,
        scratch_shapes=[
            pltpu.VMEM((128, 512), BF16),
            pltpu.VMEM((1, 512), F32),
            pltpu.VMEM((27, 16, 32), BF16),
            pltpu.VMEM((128, 512), BF16),
            *[pltpu.VMEM(table.shape, BF16) for table in tables],
            pltpu.VMEM((4, 16, 112, 128), BF16),
            pltpu.VMEM((2, 4, 4, 27, 16, 128), BF16),
            pltpu.VMEM((128, 512), BF16),
            pltpu.VMEM((128, 512), BF16),
            pltpu.VMEM((2, 96, 512), BF16),
            pltpu.VMEM((2, 96, 512), BF16),
            pltpu.VMEM((2, 64, 128), BF16),
            pltpu.VMEM((2, 64, 128), BF16),
            pltpu.VMEM((4, 384, 128), BF16),
            pltpu.VMEM((4, 384, 128), BF16),
            pltpu.VMEM((4, 4, 256, 128), BF16),
            pltpu.VMEM((3, 6, 6, 32, 128), BF16),
            pltpu.VMEM((4, 3, 6, 4, 32, 128), BF16),
            pltpu.VMEM((512, 256), F32),
            pltpu.VMEM((512, 384), F32),
            pltpu.VMEM((2, 4, 128, 256), BF16),
            pltpu.VMEM((2, 3, 128, 256), BF16),
            pltpu.VMEM((4, 128, 128), BF16),
            pltpu.VMEM((4, 128, 128), BF16),
            pltpu.VMEM((4, 64, 128), BF16),
            pltpu.VMEM((4, 64, 128), BF16),
            pltpu.VMEM((4, 128, 128), F32),
            dma((8,)),
            dma((8,)), dma((8,)),
            dma((1,)), dma((1,)),
            dma((2, 8)), dma((2, 8)),
            dma((2, 3)), dma((2, 3)),
            dma((2, 3, 2)), dma((2, 3, 2)),
            dma((2, 5)), dma((2, 5)),
            dma((5,)), dma((5,)),
            dma((4,)), dma((4,)),
            dma((2, 3)), dma((2, 3)),
            dma((3,)), dma((3,)),
            dma((4,)), dma((4,)),
        ],
        compiler_params=pltpu.CompilerParams(
            collective_id=0, has_side_effects=True, vmem_limit_bytes=40 * 1024 * 1024
        ),
        cost_estimate=pl.CostEstimate(flops=7_200_000_000, bytes_accessed=20_000_000, transcendentals=200_000),
    )(
        pin(block_input_frames.reshape(128, 512)),
        pin(norm_gain.reshape(1, 512)),
        pin(kernel.reshape(27, 16, 32)),
        pin(output_gradient.reshape(128, 512)),
        group_count,
        clip_starts,
        *[pin(table) for table in tables],
    )
    return block_out.reshape(shape), input_grad.reshape(shape)


def solution(mesh):
    frames = P("group", None, "tile", None, None, None)
    return jax.shard_map(
        per_device,
        mesh=mesh,
        in_specs=(frames, P(), P(None, None, None, "group", "tile"), frames, P("group"), P("group")),
        out_specs=(frames, frames),
        check_vma=False,
    )
```

```python
import numpy as np
import jax
import jax.numpy as jnp
from jax import lax
from jax.experimental import pallas as pl
from jax.experimental.pallas import tpu as pltpu
from jax.sharding import PartitionSpec as P

MESH = pl.DeviceIdType.MESH
EPSILON = 1e-06
F32, BF16 = jnp.float32, jnp.bfloat16


def swap_table():
    table = np.zeros((512, 512), np.float32)
    for a in range(4):
        for b in range(4):
            for o in range(32):
                table[a * 128 + b * 32 + o, b * 128 + a * 32 + o] = 1
    return table.reshape(512, 4, 128).transpose(1, 0, 2)


def column_table():
    table = np.zeros((32, 128), np.float32)
    for it in range(16):
        table[it, it * 8 + 7] = 1
        table[16 + it, it * 8] = 1
    return table


def corner_table():
    table = np.zeros((4, 64, 128), np.float32)
    for k in range(4):
        for corner, (i, j) in enumerate(((3, 7), (3, 0), (0, 7), (0, 0))):
            for t in range(4):
                table[k, 16 * corner + 4 * k + t, (i * 4 + t) * 8 + j] = 1
    return table


def edge_table():
    table = np.zeros((4, 64, 128), np.float32)
    for k in range(4):
        for side in range(2):
            for t in range(4):
                first = 16 * t + 8 * side
                table[k, first, 32 + 16 * side + 4 * k + t] = 1
                table[k, first + 5, 64 + 16 * side + 4 * k + t] = 1
                for i in range(4):
                    table[k, first + 1 + i, 16 * side + i * 4 + t] = 1
    return table


SHARDS = (0, -1, 7, -4, -7, 4, 1, -2, 6, -5, -8, 3, -3, -6, 5, 2)
CHUNKS = ((0, 1, 0), (1, 3, 0), (4, 3, 1), (7, 5, 0), (12, 4, 1))
STRIP_STEPS, COLUMN_STEPS, CORNER_STEPS = (4, -4), (1, -1), (5, 3, -3, -5)


def dot(left, right):
    return jnp.dot(left, right, preferred_element_type=F32)


def swap_lanes(value, swap_ref):
    return dot(value, jnp.concatenate([swap_ref[k] for k in range(4)], axis=1))


def body(
    x_hbm, gain_hbm, w_hbm, g_hbm, count_ref, starts_ref, swap_hbm, column_hbm, corner_hbm, edge_hbm,
    out_ref, grad_ref,
    xv, gainv, wv, gv, swap_ref, column_pick, corner_pick, edge_pick,
    wz, wbuf, tsend, trecv, rows_s, rows_r, corners_s, corners_r, amsg, abuf, gb, fbuf, bbuf,
    acc_f, acc_b, psend, precv, bsend, brecv, dsend, drecv,
    in_s, z_s, z_r, t_s, t_r, h_s, h_r, a_s, a_r, gy_s, gy_r,
    wx_s, wx_r, wf_s, wf_r, wc_s, wc_r, p_s, p_r, b_s, b_r, d_s, d_r,
):
    loads = [
        pltpu.make_async_copy(src, dst, in_s.at[k])
        for k, (src, dst) in enumerate(
            (
                (w_hbm, wv), (g_hbm, gv), (x_hbm, xv), (gain_hbm, gainv), (swap_hbm, swap_ref),
                (column_hbm, column_pick), (corner_hbm, corner_pick), (edge_hbm, edge_pick),
            )
        )
    ]
    for load in loads:
        load.start()

    group = lax.axis_index("group")
    z = lax.axis_index("tile")
    x, y, c = lax.div(group, 8), lax.rem(lax.div(group, 2), 4), lax.rem(group, 2)

    def device(x_at, y_at, c_at, z_at):
        return (x_at * 8 + y_at * 2 + c_at, z_at)

    def mod4(value):
        return lax.rem(value + 4, 4)

    def zmove(step):
        return (group, lax.rem(z + step + 16, 16))

    core = device(x, y, 1 - c, z)
    x_right, x_left = device(mod4(x + 1), y, c, z), device(mod4(x - 1), y, c, z)
    y_peers = [device(x, mod4(y + d), c, z) for d in (1, 2, 3)]
    y_right, y_left = y_peers[0], y_peers[2]
    following, previous = lax.rem(group + 1, 32), lax.rem(group + 31, 32)
    after, before = (following, z), (previous, z)
    head_targets = [(lax.rem(x * 8 + 2 * k + c + 31, 32), z) for k in range(4)]
    head_sources = [device(lax.div(following, 8), k, lax.rem(following, 2), z) for k in range(4)]

    barrier = pltpu.get_barrier_semaphore()
    partners = [core, x_right, x_left, *y_peers, after, before, *head_sources]
    partners += [zmove(step) for step in STRIP_STEPS + COLUMN_STEPS + CORNER_STEPS + (7, -7)]
    for partner in partners:
        pl.semaphore_signal(barrier, inc=1, device_id=partner, device_id_type=MESH)

    started = []

    def remote(src, dst, send_sem, recv_sem, target):
        return pltpu.make_async_remote_copy(
            src_ref=src, dst_ref=dst, send_sem=send_sem, recv_sem=recv_sem, device_id=target, device_id_type=MESH
        )

    def send(src, dst, send_sem, recv_sem, target):
        copy = remote(src, dst, send_sem, recv_sem, target)
        copy.start()
        started.append(copy)

    def arrived(dst, sem):
        remote(dst, dst, sem, sem, core).wait_recv()

    def z_first():
        for k, step in enumerate(SHARDS[1:7]):
            send(wz.at[x, 0], wz.at[x, 1 + k], z_s.at[k], z_r.at[k], zmove(-step))

    def z_first_wait():
        for k in range(6):
            arrived(wz.at[x, 1 + k], z_r.at[k])

    def z_second():
        send(wz.at[x, pl.ds(1, 5)], wz.at[x, pl.ds(7, 5)], z_s.at[6], z_r.at[6], zmove(1))
        send(wz.at[x, pl.ds(3, 4)], wz.at[x, pl.ds(12, 4)], z_s.at[7], z_r.at[7], zmove(-1))

    def z_second_wait():
        arrived(wz.at[x, pl.ds(7, 5)], z_r.at[6])
        arrived(wz.at[x, pl.ds(12, 4)], z_r.at[7])

    def x_block(step, k):
        return wz.at[mod4(x + step), pl.ds(CHUNKS[k][0], CHUNKS[k][1])]

    def x_send(k, side):
        block = x_block(0, k)
        send(block, block, wx_s.at[side, k], wx_r.at[side, k], x_left if side else x_right)

    def x_arrived(k, side):
        arrived(x_block(1 if side else -1, k), wx_r.at[side, k])

    def x_pass(k):
        side = CHUNKS[k][2]
        x_arrived(k, side)
        block = x_block(1 if side else -1, k)
        send(block, block, wf_s.at[k], wf_r.at[k], x_left if side else x_right)

    def x_far(k):
        arrived(x_block(2, k), wf_r.at[k])

    places = []
    for shard in range(16):
        away = lax.rem(shard - z + 24, 16) - 8
        place = jnp.int32(0)
        for slot in range(1, 16):
            place = jnp.where(away == SHARDS[slot], slot, place)
        places.append(place)

    def w_layout(step):
        at = mod4(x + step)
        rows = []
        for quad in range(4):
            rows.append(jnp.concatenate([wz[at, places[quad * 4 + j]] for j in range(4)], axis=1))
        full = swap_lanes(jnp.concatenate(rows, axis=0), swap_ref).astype(BF16)
        for quad in range(4):
            for tap in range(27):
                row, lanes = quad * 112 + (tap // 4) * 16, (tap % 4) * 128
                wbuf[c, at, quad, tap] = full[row : row + 16, lanes : lanes + 128]
        whole = wbuf.at[c, at]
        send(whole, whole, wc_s.at[step + 1], wc_r.at[step + 1], core)

    def w_core():
        for step in (0, -1, 1, 2):
            arrived(wbuf.at[1 - c, mod4(x + step)], wc_r.at[step + 1])

    def y_block(owner, half, part):
        return gb.at[owner, pl.ds(2 * half, 2), pl.ds(128 * part, 128)]

    def y_start(part):
        for half in range(2):
            block = y_block(y, half, part)
            send(block, block, gy_s.at[part, 0, half], gy_r.at[part, 0, half], y_right)
            send(block, block, gy_s.at[part, 1, half], gy_r.at[part, 1, half], y_left)

    def y_relay(part):
        for side, step, target in ((0, -1, y_right), (1, 1, y_left)):
            for half in (side, 1 - side):
                block = y_block(mod4(y + step), half, part)
                arrived(block, gy_r.at[part, side, half])
                if half == side:
                    send(block, block, gy_s.at[part, 2, half], gy_r.at[part, 2, half], target)

    def y_far(part):
        for half in range(2):
            arrived(y_block(mod4(y + 2), half, part), gy_r.at[part, 2, half])

    def strips_start(field, tile):
        rows_s[field, 0:32] = tile[96:128]
        rows_s[field, 32:64] = tile[0:32]
        for k, step in enumerate(STRIP_STEPS):
            block = pl.ds(32 * k, 32)
            send(rows_s.at[field, block], rows_r.at[field, block], h_s.at[field, k], h_r.at[field, k], zmove(step))

    def columns_start(field, tile):
        rows_s[field, 64:96] = dot(column_pick[...], tile).astype(BF16)
        for k, step in enumerate(COLUMN_STEPS):
            block = pl.ds(64 + 16 * k, 16)
            send(rows_s.at[field, block], rows_r.at[field, block], h_s.at[field, 2 + k], h_r.at[field, 2 + k], zmove(step))
        corners = [dot(corner_pick[k], tile[:, k * 128 : (k + 1) * 128]) for k in range(4)]
        corners_s[field] = (corners[0] + corners[1] + corners[2] + corners[3]).astype(BF16)
        for k, step in enumerate(CORNER_STEPS):
            block = pl.ds(16 * k, 16)
            send(corners_s.at[field, block], corners_r.at[field, block], h_s.at[field, 4 + k], h_r.at[field, 4 + k], zmove(step))

    tile_row, tile_column = lax.div(z, 4), lax.rem(z, 4)

    def unless(hit):
        return jnp.where(hit, 0.0, 1.0).astype(F32)

    at_top, at_bottom = unless(tile_row == 0), unless(tile_row == 3)
    at_left, at_right = unless(tile_column == 0), unless(tile_column == 3)

    def halo_finish(field):
        for k in range(2):
            arrived(rows_r.at[field, pl.ds(32 * k, 32)], h_r.at[field, k])
        for k in range(2):
            arrived(rows_r.at[field, pl.ds(64 + 16 * k, 16)], h_r.at[field, 2 + k])
        for k in range(4):
            arrived(corners_r.at[field, pl.ds(16 * k, 16)], h_r.at[field, 4 + k])
        above = rows_r[field, 0:32].astype(F32) * at_top
        below = rows_r[field, 32:64].astype(F32) * at_bottom
        row_at = lax.broadcasted_iota(jnp.int32, (64, 128), 0)
        keep = jnp.where((row_at & 8) == 0, at_left, at_right)
        keep = keep * jnp.where((row_at & 7) == 0, at_top, 1.0) * jnp.where((row_at & 7) == 5, at_bottom, 1.0)
        flag = jnp.where(row_at == 6, source, 0.0)
        edges = []
        for k in range(4):
            picks = jnp.concatenate([rows_r[field, 64:96, k * 128 : (k + 1) * 128], corners_r[field]], axis=0)
            edges.append(dot(edge_pick[k, :, 0:96], picks) * keep + flag)
        return jnp.concatenate([above, below, jnp.concatenate(edges, axis=1)], axis=0).astype(BF16)

    loads[0].wait()
    packed = jnp.zeros((112, 128), F32)
    for k in range(4):
        taps = [wv[4 * row + k] if 4 * row + k < 27 else jnp.zeros((16, 32), BF16) for row in range(7)]
        lane_at = lax.broadcasted_iota(jnp.int32, (32, 128), 1) - lax.broadcasted_iota(jnp.int32, (32, 128), 0)
        packed = packed + dot(jnp.concatenate(taps, axis=0), jnp.where(lane_at == 32 * k, 1.0, 0.0).astype(BF16))
    wz[x, 0] = packed.astype(BF16)

    live = jnp.where(count_ref[0] > 0, 1.0, 0.0).astype(F32)
    fresh = jnp.where(starts_ref[0] == 0, 1.0, 0.0).astype(F32)
    source = live * fresh * jnp.where(group > 0, 1.0, 0.0).astype(F32)

    def swap_frames(value):
        value = value.reshape(4, 4, 8, value.shape[1])
        return jnp.concatenate([value[:, k] for k in range(4)], axis=0).reshape(128, value.shape[3])

    loads[1].wait()
    masked = gv[...].astype(F32) * live
    grad_tile = swap_frames(masked).astype(BF16)
    for k in range(4):
        gb[y, k, 0:128] = grad_tile[:, k * 128 : (k + 1) * 128]

    pl.semaphore_wait(barrier, len(partners))
    z_first()
    x_send(0, 0)
    x_send(0, 1)
    y_start(0)

    loads[2].wait()
    loads[3].wait()
    loads[4].wait()
    gain = gainv[...]
    values = xv[...].astype(F32)
    scale = lax.rsqrt(jnp.mean(values * values, axis=-1, keepdims=True) + EPSILON)
    normed = values * scale * gain
    activated = (normed * jax.nn.sigmoid(normed)).astype(BF16)
    swapped = swap_lanes(activated, swap_ref)
    tsend[0:64] = swapped[64:128].astype(BF16)
    act_tile = swap_frames(swapped).astype(BF16)

    def a_rows(part):
        return pl.ds(0, 128) if part == 0 else pl.ds(128, 256)

    def a_start(part, value):
        first = 0 if part == 0 else 128
        for k in range(4):
            amsg[k, first : first + value.shape[0]] = value[:, k * 128 : (k + 1) * 128]
        for d in (1, 2, 3):
            src, dst = amsg.at[mod4(y + d), a_rows(part)], abuf.at[y, a_rows(part)]
            send(src, dst, a_s.at[part, d - 1], a_r.at[part, d - 1], y_peers[d - 1])
        abuf[y, first : first + value.shape[0]] = amsg[y, first : first + value.shape[0]]

    def a_wait(part):
        for d in (1, 2, 3):
            arrived(abuf.at[mod4(y - d), a_rows(part)], a_r.at[part, d - 1])

    a_start(0, act_tile)
    for load in loads[5:]:
        load.wait()
    strips_start(0, act_tile)
    columns_start(0, act_tile)
    z_first_wait()
    z_second()
    for k, side in ((1, 0), (2, 1), (2, 0), (1, 1)):
        x_send(k, side)
    x_pass(0)
    strips_start(1, grad_tile)
    columns_start(1, grad_tile)
    y_relay(0)
    halo = halo_finish(0)
    tsend[64:80] = halo[16:32]
    tsend[80:96] = halo[48:64]
    tsend[96:128] = halo[96:128]
    send(tsend, trecv, t_s.at[0], t_r.at[0], after)
    z_second_wait()
    for k, side in ((3, 0), (4, 1), (4, 0), (3, 1)):
        x_send(k, side)
    x_pass(1)
    x_pass(2)
    w_layout(0)
    arrived(trecv, t_r.at[0])
    a_start(1, jnp.concatenate([halo, (trecv[...].astype(F32) * source).astype(BF16)], axis=0))
    grad_halo = halo_finish(1)
    for k in range(4):
        gb[y, k, 128:256] = grad_halo[:, k * 128 : (k + 1) * 128]
    y_start(1)
    x_pass(3)
    x_pass(4)
    for k in range(5):
        x_arrived(k, 1 - CHUNKS[k][2])
    w_layout(-1)
    w_layout(1)
    y_relay(1)

    def shifted(slabs, centers, edges):
        center = jnp.concatenate([slabs[k : k + 1] for k in centers], axis=0)
        sides = []
        for side in range(2):
            rows = [jnp.broadcast_to(slabs[k + side, i : i + 1], slabs.shape[1:])[None] for k, i in edges]
            sides.append(jnp.concatenate(rows, axis=0))
        at = lax.broadcasted_iota(jnp.int32, center.shape, 1)
        from_left = jnp.where(at == 0, sides[0], pltpu.roll(center, 1, 1))
        from_right = jnp.where(at == 7, sides[1], pltpu.roll(center, 7, 1))
        return from_left, center, from_right

    def own_slab(i, t):
        return 16 + t if i == 0 else 20 + t if i == 5 else (i - 1) * 4 + t

    def carried_slab(i, t):
        return 40 + t if i == 0 else 42 + t if i == 5 else 32 + t * 4 + i - 1

    grad_centers = [own_slab(i, t) for i in range(6) for t in range(4)]
    grad_edges = [(24 + 2 * t, i) for i in range(6) for t in range(4)]
    act_centers = [carried_slab(i, t) if t < 2 else own_slab(i, t - 2) for i in range(6) for t in range(6)]
    act_edges = [(44 + 2 * t, i) if t < 2 else (24 + 2 * (t - 2), i) for i in range(6) for t in range(6)]

    a_wait(0)
    a_wait(1)

    def build_f(pair, carry):
        parts = []
        for k in range(2):
            slabs = abuf[2 * pair + k].astype(F32).reshape(48, 8, 128)
            parts.append(shifted(slabs, act_centers, act_edges))
        rows = pl.ds(pl.multiple_of(16 * pair, 16), 16)
        for e in range(3):
            value = jnp.concatenate([part[e] for part in parts], axis=1).astype(BF16)
            fbuf[e, :, :, rows] = value.reshape(6, 6, 16, 128)
        return carry

    lax.fori_loop(0, 2, build_f, 0)

    def build_g(k, carry):
        half, pair = lax.div(k, 2), lax.rem(k, 2)
        parts = []
        for n in range(2):
            message = jnp.concatenate([gb[2 * pair + n, 2 * half + m] for m in range(2)], axis=1)
            parts.append(shifted(message.astype(F32).reshape(32, 8, 256), grad_centers, grad_edges))
        rows = pl.ds(pl.multiple_of(16 * pair, 16), 16)
        for e in range(3):
            value = jnp.concatenate([part[e] for part in parts], axis=1).astype(BF16)
            for m in range(2):
                bbuf[2 * half + m, e, :, :, rows] = value[:, :, m * 128 : (m + 1) * 128].reshape(6, 4, 16, 128)
        return carry

    def taps_of(r, tap):
        return jnp.concatenate([wbuf[k, i, r, tap] for i in range(4) for k in range(2)], axis=0)

    def forward():
        acc_f[...] = jnp.zeros_like(acc_f)

        def frame_tap(a, carry):
            windows, taps = [], []
            for b in range(3):
                for e in range(3):
                    windows.append(fbuf[e, b : b + 4, pl.ds(a, 4)].reshape(512, 128))
                    tap = a * 9 + b * 3 + e
                    taps.append(jnp.concatenate([taps_of(quad, tap) for quad in range(4)], axis=1))
            acc_f[...] += dot(jnp.concatenate(windows, axis=1), jnp.concatenate(taps, axis=0))
            return carry

        lax.fori_loop(0, 3, frame_tap, 0)
        total = acc_f[...].reshape(16, 32, 512)
        for other in range(4):
            psend[other] = total[:, other * 8 : other * 8 + 8].reshape(128, 512).astype(BF16)
        for d in (1, 2, 3):
            send(psend.at[mod4(y + d)], precv.at[d - 1], p_s.at[d - 1], p_r.at[d - 1], y_peers[d - 1])

    def backward():
        acc_b[...] = jnp.zeros_like(acc_b)

        def row_tap(b, carry):
            windows, taps = [], []
            for e in range(3):
                for quad in range(4):
                    windows.append(bbuf[quad, 2 - e, pl.ds(2 - b, 4)].reshape(512, 128))
                    taps.append(jnp.concatenate([taps_of(quad, a * 9 + b * 3 + e) for a in range(3)], axis=0))
            acc_b[...] += lax.dot_general(
                jnp.concatenate(windows, axis=1),
                jnp.concatenate(taps, axis=1),
                (((1,), (1,)), ((), ())),
                preferred_element_type=F32,
            )
            return carry

        lax.fori_loop(0, 3, row_tap, 0)

    sigma = jax.nn.sigmoid(normed)
    slope = sigma * (1.0 + normed * (1.0 - sigma)) * gain
    y_far(0)
    y_far(1)
    lax.fori_loop(0, 4, build_g, 0)
    for k in range(5):
        x_far(k)
    w_layout(2)
    w_core()
    forward()
    backward()
    taps = acc_b[...].reshape(4, 4, 32, 384)
    spread = []
    for u in range(6):
        terms = [taps[:, u - a, :, a * 128 : (a + 1) * 128] for a in range(3) if 0 <= u - a < 4]
        spread.append(sum(terms[1:], terms[0]))
    for other in range(4):
        slots = [part[:, other * 8 : other * 8 + 8] for part in spread]
        bsend[other] = jnp.stack(slots[2:], axis=1).reshape(128, 128).astype(BF16)
        flag = gb[other, 0, 192:208].astype(F32)[6:7]
        dsend[other] = (jnp.stack(slots[:2], axis=1).reshape(64, 128) * flag).astype(BF16)
    for d in (1, 2, 3):
        send(bsend.at[mod4(y + d)], brecv.at[y], b_s.at[d - 1], b_r.at[d - 1], y_peers[d - 1])
    for k in range(4):
        send(dsend.at[k], drecv.at[y], d_s.at[k], d_r.at[y], head_targets[k])
    brecv[y] = bsend[y]
    mixed = psend[y].astype(F32)
    for d in (1, 2, 3):
        arrived(precv.at[d - 1], p_r.at[d - 1])
        mixed = mixed + precv[d - 1].astype(F32)
    out_ref[...] = ((values + swap_frames(mixed)) * live).astype(BF16)
    for copy in started[:-7]:
        copy.wait_send()
    for d in (1, 2, 3):
        arrived(brecv.at[mod4(y - d)], b_r.at[d - 1])
    for k in range(4):
        arrived(drecv.at[k], d_r.at[k])
    own = jnp.concatenate([brecv[k] for k in range(4)], axis=1).astype(F32).reshape(4, 4, 8, 512)
    heads = jnp.concatenate([drecv[k] for k in range(4)], axis=1).astype(F32).reshape(4, 2, 8, 512)
    upstream = swap_lanes(own.reshape(128, 512).astype(BF16), swap_ref).reshape(4, 4, 8, 512)
    tails = swap_lanes(heads.reshape(64, 512).astype(BF16), swap_ref).reshape(4, 2, 8, 512)
    upstream = jnp.concatenate(
        [upstream[:, 0], upstream[:, 1], upstream[:, 2] + tails[:, 0], upstream[:, 3] + tails[:, 1]], axis=0
    ).reshape(128, 512)
    through = upstream * slope
    cubed = scale * scale * scale
    through_mean = jnp.mean(values * through, axis=-1, keepdims=True)
    gradient = masked + scale * through - values * cubed * through_mean
    grad_ref[...] = (gradient * live).astype(BF16)
    for copy in started[-7:]:
        copy.wait_send()


def pin(value):
    return pltpu.with_memory_space_constraint(value, pltpu.HBM)


def per_device(block_input_frames, norm_gain, kernel, output_gradient, group_count, clip_starts):
    shape = block_input_frames.shape
    tables = [jnp.asarray(table(), BF16) for table in (swap_table, column_table, corner_table, edge_table)]
    vmem, smem, hbm = [pl.BlockSpec(memory_space=space) for space in (pltpu.VMEM, pltpu.SMEM, pltpu.HBM)]
    dma = pltpu.SemaphoreType.DMA
    block_out, input_grad = pl.pallas_call(
        body,
        out_shape=[jax.ShapeDtypeStruct((128, 512), BF16)] * 2,
        in_specs=[hbm] * 4 + [smem] * 2 + [hbm] * 4,
        out_specs=[vmem] * 2,
        scratch_shapes=[
            pltpu.VMEM((128, 512), BF16),
            pltpu.VMEM((1, 512), F32),
            pltpu.VMEM((27, 16, 32), BF16),
            pltpu.VMEM((128, 512), BF16),
            *[pltpu.VMEM(table.shape, BF16) for table in tables],
            pltpu.VMEM((4, 16, 112, 128), BF16),
            pltpu.VMEM((2, 4, 4, 27, 16, 128), BF16),
            pltpu.VMEM((128, 512), BF16),
            pltpu.VMEM((128, 512), BF16),
            pltpu.VMEM((2, 96, 512), BF16),
            pltpu.VMEM((2, 96, 512), BF16),
            pltpu.VMEM((2, 64, 128), BF16),
            pltpu.VMEM((2, 64, 128), BF16),
            pltpu.VMEM((4, 384, 128), BF16),
            pltpu.VMEM((4, 384, 128), BF16),
            pltpu.VMEM((4, 4, 256, 128), BF16),
            pltpu.VMEM((3, 6, 6, 32, 128), BF16),
            pltpu.VMEM((4, 3, 6, 4, 32, 128), BF16),
            pltpu.VMEM((512, 512), F32),
            pltpu.VMEM((512, 384), F32),
            pltpu.VMEM((4, 128, 512), BF16),
            pltpu.VMEM((3, 128, 512), BF16),
            pltpu.VMEM((4, 128, 128), BF16),
            pltpu.VMEM((4, 128, 128), BF16),
            pltpu.VMEM((4, 64, 128), BF16),
            pltpu.VMEM((4, 64, 128), BF16),
            dma((8,)),
            dma((8,)), dma((8,)),
            dma((1,)), dma((1,)),
            dma((2, 8)), dma((2, 8)),
            dma((2, 3)), dma((2, 3)),
            dma((2, 3, 2)), dma((2, 3, 2)),
            dma((2, 5)), dma((2, 5)),
            dma((5,)), dma((5,)),
            dma((4,)), dma((4,)),
            dma((3,)), dma((3,)),
            dma((3,)), dma((3,)),
            dma((4,)), dma((4,)),
        ],
        compiler_params=pltpu.CompilerParams(
            collective_id=0, has_side_effects=True, vmem_limit_bytes=40 * 1024 * 1024
        ),
        cost_estimate=pl.CostEstimate(flops=7_200_000_000, bytes_accessed=20_000_000, transcendentals=200_000),
    )(
        pin(block_input_frames.reshape(128, 512)),
        pin(norm_gain.reshape(1, 512)),
        pin(kernel.reshape(27, 16, 32)),
        pin(output_gradient.reshape(128, 512)),
        group_count,
        clip_starts,
        *[pin(table) for table in tables],
    )
    return block_out.reshape(shape), input_grad.reshape(shape)


def solution(mesh):
    frames = P("group", None, "tile", None, None, None)
    return jax.shard_map(
        per_device,
        mesh=mesh,
        in_specs=(frames, P(), P(None, None, None, "group", "tile"), frames, P("group"), P("group")),
        out_specs=(frames, frames),
        check_vma=False,
    )
```

```python
import numpy as np
import jax
import jax.numpy as jnp
from jax import lax
from jax.experimental import pallas as pl
from jax.experimental.pallas import tpu as pltpu
from jax.sharding import PartitionSpec as P

MESH = pl.DeviceIdType.MESH
EPSILON = 1e-06
F32, BF16 = jnp.float32, jnp.bfloat16


def swap_table():
    table = np.zeros((512, 512), np.float32)
    for a in range(4):
        for b in range(4):
            for o in range(32):
                table[a * 128 + b * 32 + o, b * 128 + a * 32 + o] = 1
    return table.reshape(512, 4, 128).transpose(1, 0, 2)


def column_table():
    table = np.zeros((32, 128), np.float32)
    for it in range(16):
        table[it, it * 8 + 7] = 1
        table[16 + it, it * 8] = 1
    return table


def corner_table():
    table = np.zeros((4, 64, 128), np.float32)
    for k in range(4):
        for corner, (i, j) in enumerate(((3, 7), (3, 0), (0, 7), (0, 0))):
            for t in range(4):
                table[k, 16 * corner + 4 * k + t, (i * 4 + t) * 8 + j] = 1
    return table


def edge_table():
    table = np.zeros((4, 64, 128), np.float32)
    for k in range(4):
        for side in range(2):
            for t in range(4):
                first = 16 * t + 8 * side
                table[k, first, 32 + 16 * side + 4 * k + t] = 1
                table[k, first + 5, 64 + 16 * side + 4 * k + t] = 1
                for i in range(4):
                    table[k, first + 1 + i, 16 * side + i * 4 + t] = 1
    return table


SHARDS = (0, -1, 7, -4, -7, 4, 1, -2, 6, -5, -8, 3, -3, -6, 5, 2)
CHUNKS = ((0, 1, 0), (1, 3, 0), (4, 3, 1), (7, 5, 0), (12, 4, 1))
STRIP_STEPS, COLUMN_STEPS, CORNER_STEPS = (4, -4), (1, -1), (5, 3, -3, -5)


def dot(left, right):
    return jnp.dot(left, right, preferred_element_type=F32)


def swap_lanes(value, swap_ref):
    return dot(value, jnp.concatenate([swap_ref[k] for k in range(4)], axis=1))


def body(
    x_hbm, gain_hbm, w_hbm, g_hbm, count_ref, starts_ref, swap_hbm, column_hbm, corner_hbm, edge_hbm,
    out_ref, grad_ref,
    xv, gainv, wv, gv, swap_ref, column_pick, corner_pick, edge_pick,
    wz, wbuf, tsend, trecv, rows_s, rows_r, corners_s, corners_r, amsg, abuf, gb, fbuf, bbuf,
    acc_f, acc_b, psend, precv, bsend, brecv, dsend, drecv,
    in_s, z_s, z_r, t_s, t_r, h_s, h_r, a_s, a_r, gy_s, gy_r,
    wx_s, wx_r, wf_s, wf_r, wc_s, wc_r, p_s, p_r, b_s, b_r, d_s, d_r,
):
    loads = [
        pltpu.make_async_copy(src, dst, in_s.at[k])
        for k, (src, dst) in enumerate(
            (
                (w_hbm, wv), (g_hbm, gv), (x_hbm, xv), (gain_hbm, gainv), (swap_hbm, swap_ref),
                (column_hbm, column_pick), (corner_hbm, corner_pick), (edge_hbm, edge_pick),
            )
        )
    ]
    for load in loads:
        load.start()

    group = lax.axis_index("group")
    z = lax.axis_index("tile")
    x, y, c = lax.div(group, 8), lax.rem(lax.div(group, 2), 4), lax.rem(group, 2)

    def device(x_at, y_at, c_at, z_at):
        return (x_at * 8 + y_at * 2 + c_at, z_at)

    def mod4(value):
        return lax.rem(value + 4, 4)

    def zmove(step):
        return (group, lax.rem(z + step + 16, 16))

    core = device(x, y, 1 - c, z)
    x_right, x_left = device(mod4(x + 1), y, c, z), device(mod4(x - 1), y, c, z)
    y_peers = [device(x, mod4(y + d), c, z) for d in (1, 2, 3)]
    y_right, y_left = y_peers[0], y_peers[2]
    following, previous = lax.rem(group + 1, 32), lax.rem(group + 31, 32)
    after, before = (following, z), (previous, z)
    head_targets = [(lax.rem(x * 8 + 2 * k + c + 31, 32), z) for k in range(4)]
    head_sources = [device(lax.div(following, 8), k, lax.rem(following, 2), z) for k in range(4)]

    barrier = pltpu.get_barrier_semaphore()
    partners = [core, x_right, x_left, *y_peers, after, before, *head_sources]
    partners += [zmove(step) for step in STRIP_STEPS + COLUMN_STEPS + CORNER_STEPS + (7, -7)]
    for partner in partners:
        pl.semaphore_signal(barrier, inc=1, device_id=partner, device_id_type=MESH)

    started = []

    def remote(src, dst, send_sem, recv_sem, target):
        return pltpu.make_async_remote_copy(
            src_ref=src, dst_ref=dst, send_sem=send_sem, recv_sem=recv_sem, device_id=target, device_id_type=MESH
        )

    def send(src, dst, send_sem, recv_sem, target):
        copy = remote(src, dst, send_sem, recv_sem, target)
        copy.start()
        started.append(copy)

    def arrived(dst, sem):
        remote(dst, dst, sem, sem, core).wait_recv()

    def z_first():
        for k, step in enumerate(SHARDS[1:7]):
            send(wz.at[x, 0], wz.at[x, 1 + k], z_s.at[k], z_r.at[k], zmove(-step))

    def z_first_wait():
        for k in range(6):
            arrived(wz.at[x, 1 + k], z_r.at[k])

    def z_second():
        send(wz.at[x, pl.ds(1, 5)], wz.at[x, pl.ds(7, 5)], z_s.at[6], z_r.at[6], zmove(1))
        send(wz.at[x, pl.ds(3, 4)], wz.at[x, pl.ds(12, 4)], z_s.at[7], z_r.at[7], zmove(-1))

    def z_second_wait():
        arrived(wz.at[x, pl.ds(7, 5)], z_r.at[6])
        arrived(wz.at[x, pl.ds(12, 4)], z_r.at[7])

    def x_block(step, k):
        return wz.at[mod4(x + step), pl.ds(CHUNKS[k][0], CHUNKS[k][1])]

    def x_send(k, side):
        block = x_block(0, k)
        send(block, block, wx_s.at[side, k], wx_r.at[side, k], x_left if side else x_right)

    def x_arrived(k, side):
        arrived(x_block(1 if side else -1, k), wx_r.at[side, k])

    def x_pass(k):
        side = CHUNKS[k][2]
        x_arrived(k, side)
        block = x_block(1 if side else -1, k)
        send(block, block, wf_s.at[k], wf_r.at[k], x_left if side else x_right)

    def x_far(k):
        arrived(x_block(2, k), wf_r.at[k])

    places = []
    for shard in range(16):
        away = lax.rem(shard - z + 24, 16) - 8
        place = jnp.int32(0)
        for slot in range(1, 16):
            place = jnp.where(away == SHARDS[slot], slot, place)
        places.append(place)

    def w_layout(step):
        at = mod4(x + step)
        rows = []
        for quad in range(4):
            rows.append(jnp.concatenate([wz[at, places[quad * 4 + j]] for j in range(4)], axis=1))
        full = swap_lanes(jnp.concatenate(rows, axis=0), swap_ref).astype(BF16)
        for quad in range(4):
            for tap in range(27):
                row, lanes = quad * 112 + (tap // 4) * 16, (tap % 4) * 128
                wbuf[c, at, quad, tap] = full[row : row + 16, lanes : lanes + 128]
        whole = wbuf.at[c, at]
        send(whole, whole, wc_s.at[step + 1], wc_r.at[step + 1], core)

    def w_core():
        for step in (0, -1, 1, 2):
            arrived(wbuf.at[1 - c, mod4(x + step)], wc_r.at[step + 1])

    def y_block(owner, half, part):
        return gb.at[owner, pl.ds(2 * half, 2), pl.ds(128 * part, 128)]

    def y_start(part):
        for half in range(2):
            block = y_block(y, half, part)
            send(block, block, gy_s.at[part, 0, half], gy_r.at[part, 0, half], y_right)
            send(block, block, gy_s.at[part, 1, half], gy_r.at[part, 1, half], y_left)

    def y_relay(part):
        for side, step, target in ((0, -1, y_right), (1, 1, y_left)):
            for half in (side, 1 - side):
                block = y_block(mod4(y + step), half, part)
                arrived(block, gy_r.at[part, side, half])
                if half == side:
                    send(block, block, gy_s.at[part, 2, half], gy_r.at[part, 2, half], target)

    def y_far(part):
        for half in range(2):
            arrived(y_block(mod4(y + 2), half, part), gy_r.at[part, 2, half])

    def strips_start(field, tile):
        rows_s[field, 0:32] = tile[96:128]
        rows_s[field, 32:64] = tile[0:32]
        for k, step in enumerate(STRIP_STEPS):
            block = pl.ds(32 * k, 32)
            send(rows_s.at[field, block], rows_r.at[field, block], h_s.at[field, k], h_r.at[field, k], zmove(step))

    def columns_start(field, tile):
        rows_s[field, 64:96] = dot(column_pick[...], tile).astype(BF16)
        for k, step in enumerate(COLUMN_STEPS):
            block = pl.ds(64 + 16 * k, 16)
            send(rows_s.at[field, block], rows_r.at[field, block], h_s.at[field, 2 + k], h_r.at[field, 2 + k], zmove(step))
        corners = [dot(corner_pick[k], tile[:, k * 128 : (k + 1) * 128]) for k in range(4)]
        corners_s[field] = (corners[0] + corners[1] + corners[2] + corners[3]).astype(BF16)
        for k, step in enumerate(CORNER_STEPS):
            block = pl.ds(16 * k, 16)
            send(corners_s.at[field, block], corners_r.at[field, block], h_s.at[field, 4 + k], h_r.at[field, 4 + k], zmove(step))

    tile_row, tile_column = lax.div(z, 4), lax.rem(z, 4)

    def unless(hit):
        return jnp.where(hit, 0.0, 1.0).astype(F32)

    at_top, at_bottom = unless(tile_row == 0), unless(tile_row == 3)
    at_left, at_right = unless(tile_column == 0), unless(tile_column == 3)

    def halo_finish(field):
        for k in range(2):
            arrived(rows_r.at[field, pl.ds(32 * k, 32)], h_r.at[field, k])
        for k in range(2):
            arrived(rows_r.at[field, pl.ds(64 + 16 * k, 16)], h_r.at[field, 2 + k])
        for k in range(4):
            arrived(corners_r.at[field, pl.ds(16 * k, 16)], h_r.at[field, 4 + k])
        above = rows_r[field, 0:32].astype(F32) * at_top
        below = rows_r[field, 32:64].astype(F32) * at_bottom
        row_at = lax.broadcasted_iota(jnp.int32, (64, 128), 0)
        keep = jnp.where((row_at & 8) == 0, at_left, at_right)
        keep = keep * jnp.where((row_at & 7) == 0, at_top, 1.0) * jnp.where((row_at & 7) == 5, at_bottom, 1.0)
        flag = jnp.where(row_at == 6, source, 0.0)
        edges = []
        for k in range(4):
            picks = jnp.concatenate([rows_r[field, 64:96, k * 128 : (k + 1) * 128], corners_r[field]], axis=0)
            edges.append(dot(edge_pick[k, :, 0:96], picks) * keep + flag)
        return jnp.concatenate([above, below, jnp.concatenate(edges, axis=1)], axis=0).astype(BF16)

    loads[0].wait()
    packed = jnp.zeros((112, 128), F32)
    for k in range(4):
        taps = [wv[4 * row + k] if 4 * row + k < 27 else jnp.zeros((16, 32), BF16) for row in range(7)]
        lane_at = lax.broadcasted_iota(jnp.int32, (32, 128), 1) - lax.broadcasted_iota(jnp.int32, (32, 128), 0)
        packed = packed + dot(jnp.concatenate(taps, axis=0), jnp.where(lane_at == 32 * k, 1.0, 0.0).astype(BF16))
    wz[x, 0] = packed.astype(BF16)

    live = jnp.where(count_ref[0] > 0, 1.0, 0.0).astype(F32)
    fresh = jnp.where(starts_ref[0] == 0, 1.0, 0.0).astype(F32)
    source = live * fresh * jnp.where(group > 0, 1.0, 0.0).astype(F32)

    def swap_frames(value):
        value = value.reshape(4, 4, 8, value.shape[1])
        return jnp.concatenate([value[:, k] for k in range(4)], axis=0).reshape(128, value.shape[3])

    loads[1].wait()
    masked = gv[...].astype(F32) * live
    grad_tile = swap_frames(masked).astype(BF16)
    for k in range(4):
        gb[y, k, 0:128] = grad_tile[:, k * 128 : (k + 1) * 128]

    pl.semaphore_wait(barrier, len(partners))
    z_first()
    x_send(0, 0)
    x_send(0, 1)
    y_start(0)

    loads[2].wait()
    loads[3].wait()
    loads[4].wait()
    gain = gainv[...]
    values = xv[...].astype(F32)
    scale = lax.rsqrt(jnp.mean(values * values, axis=-1, keepdims=True) + EPSILON)
    normed = values * scale * gain
    activated = (normed * jax.nn.sigmoid(normed)).astype(BF16)
    swapped = swap_lanes(activated, swap_ref)
    tsend[0:64] = swapped[64:128].astype(BF16)
    act_tile = swap_frames(swapped).astype(BF16)

    def a_rows(part):
        return pl.ds(0, 128) if part == 0 else pl.ds(128, 256)

    def a_start(part, value):
        first = 0 if part == 0 else 128
        for k in range(4):
            amsg[k, first : first + value.shape[0]] = value[:, k * 128 : (k + 1) * 128]
        for d in (1, 2, 3):
            src, dst = amsg.at[mod4(y + d), a_rows(part)], abuf.at[y, a_rows(part)]
            send(src, dst, a_s.at[part, d - 1], a_r.at[part, d - 1], y_peers[d - 1])
        abuf[y, first : first + value.shape[0]] = amsg[y, first : first + value.shape[0]]

    def a_wait(part):
        for d in (1, 2, 3):
            arrived(abuf.at[mod4(y - d), a_rows(part)], a_r.at[part, d - 1])

    a_start(0, act_tile)
    for load in loads[5:]:
        load.wait()
    strips_start(0, act_tile)
    columns_start(0, act_tile)
    z_first_wait()
    z_second()
    for k, side in ((1, 0), (2, 1), (2, 0), (1, 1)):
        x_send(k, side)
    strips_start(1, grad_tile)
    columns_start(1, grad_tile)
    x_pass(0)
    y_relay(0)
    halo = halo_finish(0)
    tsend[64:80] = halo[16:32]
    tsend[80:96] = halo[48:64]
    tsend[96:128] = halo[96:128]
    send(tsend, trecv, t_s.at[0], t_r.at[0], after)
    z_second_wait()
    for k, side in ((3, 0), (4, 1), (4, 0), (3, 1)):
        x_send(k, side)
    grad_halo = halo_finish(1)
    for k in range(4):
        gb[y, k, 128:256] = grad_halo[:, k * 128 : (k + 1) * 128]
    y_start(1)
    x_pass(1)
    x_pass(2)
    w_layout(0)
    arrived(trecv, t_r.at[0])
    a_start(1, jnp.concatenate([halo, (trecv[...].astype(F32) * source).astype(BF16)], axis=0))
    x_pass(3)
    x_pass(4)
    y_relay(1)
    for k in range(5):
        x_arrived(k, 1 - CHUNKS[k][2])
    w_layout(-1)
    w_layout(1)

    def shifted(slabs, centers, edges):
        center = jnp.concatenate([slabs[k : k + 1] for k in centers], axis=0)
        sides = []
        for side in range(2):
            rows = [jnp.broadcast_to(slabs[k + side, i : i + 1], slabs.shape[1:])[None] for k, i in edges]
            sides.append(jnp.concatenate(rows, axis=0))
        at = lax.broadcasted_iota(jnp.int32, center.shape, 1)
        from_left = jnp.where(at == 0, sides[0], pltpu.roll(center, 1, 1))
        from_right = jnp.where(at == 7, sides[1], pltpu.roll(center, 7, 1))
        return from_left, center, from_right

    def own_slab(i, t):
        return 16 + t if i == 0 else 20 + t if i == 5 else (i - 1) * 4 + t

    def carried_slab(i, t):
        return 40 + t if i == 0 else 42 + t if i == 5 else 32 + t * 4 + i - 1

    grad_centers = [own_slab(i, t) for i in range(6) for t in range(4)]
    grad_edges = [(24 + 2 * t, i) for i in range(6) for t in range(4)]
    act_centers = [carried_slab(i, t) if t < 2 else own_slab(i, t - 2) for i in range(6) for t in range(6)]
    act_edges = [(44 + 2 * t, i) if t < 2 else (24 + 2 * (t - 2), i) for i in range(6) for t in range(6)]

    a_wait(0)
    a_wait(1)

    def build_f(pair, carry):
        parts = []
        for k in range(2):
            slabs = abuf[2 * pair + k].astype(F32).reshape(48, 8, 128)
            parts.append(shifted(slabs, act_centers, act_edges))
        rows = pl.ds(pl.multiple_of(16 * pair, 16), 16)
        for e in range(3):
            value = jnp.concatenate([part[e] for part in parts], axis=1).astype(BF16)
            fbuf[e, :, :, rows] = value.reshape(6, 6, 16, 128)
        return carry

    lax.fori_loop(0, 2, build_f, 0)

    def build_g(k, carry):
        half, pair = lax.div(k, 2), lax.rem(k, 2)
        parts = []
        for n in range(2):
            message = jnp.concatenate([gb[2 * pair + n, 2 * half + m] for m in range(2)], axis=1)
            parts.append(shifted(message.astype(F32).reshape(32, 8, 256), grad_centers, grad_edges))
        rows = pl.ds(pl.multiple_of(16 * pair, 16), 16)
        for e in range(3):
            value = jnp.concatenate([part[e] for part in parts], axis=1).astype(BF16)
            for m in range(2):
                bbuf[2 * half + m, e, :, :, rows] = value[:, :, m * 128 : (m + 1) * 128].reshape(6, 4, 16, 128)
        return carry

    def taps_of(r, tap):
        return jnp.concatenate([wbuf[k, i, r, tap] for i in range(4) for k in range(2)], axis=0)

    def forward():
        acc_f[...] = jnp.zeros_like(acc_f)

        def frame_tap(a, carry):
            windows, taps = [], []
            for b in range(3):
                for e in range(3):
                    windows.append(fbuf[e, b : b + 4, pl.ds(a, 4)].reshape(512, 128))
                    tap = a * 9 + b * 3 + e
                    taps.append(jnp.concatenate([taps_of(quad, tap) for quad in range(4)], axis=1))
            acc_f[...] += dot(jnp.concatenate(windows, axis=1), jnp.concatenate(taps, axis=0))
            return carry

        lax.fori_loop(0, 3, frame_tap, 0)
        total = acc_f[...].reshape(16, 32, 512)
        for other in range(4):
            psend[other] = total[:, other * 8 : other * 8 + 8].reshape(128, 512).astype(BF16)
        for d in (1, 2, 3):
            send(psend.at[mod4(y + d)], precv.at[d - 1], p_s.at[d - 1], p_r.at[d - 1], y_peers[d - 1])

    def backward():
        acc_b[...] = jnp.zeros_like(acc_b)

        def row_tap(b, carry):
            windows, taps = [], []
            for e in range(3):
                for quad in range(4):
                    windows.append(bbuf[quad, 2 - e, pl.ds(2 - b, 4)].reshape(512, 128))
                    taps.append(jnp.concatenate([taps_of(quad, a * 9 + b * 3 + e) for a in range(3)], axis=0))
            acc_b[...] += lax.dot_general(
                jnp.concatenate(windows, axis=1),
                jnp.concatenate(taps, axis=1),
                (((1,), (1,)), ((), ())),
                preferred_element_type=F32,
            )
            return carry

        lax.fori_loop(0, 3, row_tap, 0)

    sigma = jax.nn.sigmoid(normed)
    slope = sigma * (1.0 + normed * (1.0 - sigma)) * gain
    for k in range(5):
        x_far(k)
    w_layout(2)
    y_far(0)
    y_far(1)
    lax.fori_loop(0, 4, build_g, 0)
    w_core()
    forward()
    backward()
    taps = acc_b[...].reshape(4, 4, 32, 384)
    spread = []
    for u in range(6):
        terms = [taps[:, u - a, :, a * 128 : (a + 1) * 128] for a in range(3) if 0 <= u - a < 4]
        spread.append(sum(terms[1:], terms[0]))
    for other in range(4):
        slots = [part[:, other * 8 : other * 8 + 8] for part in spread]
        bsend[other] = jnp.stack(slots[2:], axis=1).reshape(128, 128).astype(BF16)
        flag = gb[other, 0, 192:208].astype(F32)[6:7]
        dsend[other] = (jnp.stack(slots[:2], axis=1).reshape(64, 128) * flag).astype(BF16)
    for d in (1, 2, 3):
        send(bsend.at[mod4(y + d)], brecv.at[y], b_s.at[d - 1], b_r.at[d - 1], y_peers[d - 1])
    for k in range(4):
        send(dsend.at[k], drecv.at[y], d_s.at[k], d_r.at[y], head_targets[k])
    brecv[y] = bsend[y]
    mixed = psend[y].astype(F32)
    for d in (1, 2, 3):
        arrived(precv.at[d - 1], p_r.at[d - 1])
        mixed = mixed + precv[d - 1].astype(F32)
    out_ref[...] = ((values + swap_frames(mixed)) * live).astype(BF16)
    for copy in started[:-7]:
        copy.wait_send()
    for d in (1, 2, 3):
        arrived(brecv.at[mod4(y - d)], b_r.at[d - 1])
    for k in range(4):
        arrived(drecv.at[k], d_r.at[k])
    own = jnp.concatenate([brecv[k] for k in range(4)], axis=1).astype(F32).reshape(4, 4, 8, 512)
    heads = jnp.concatenate([drecv[k] for k in range(4)], axis=1).astype(F32).reshape(4, 2, 8, 512)
    upstream = swap_lanes(own.reshape(128, 512).astype(BF16), swap_ref).reshape(4, 4, 8, 512)
    tails = swap_lanes(heads.reshape(64, 512).astype(BF16), swap_ref).reshape(4, 2, 8, 512)
    upstream = jnp.concatenate(
        [upstream[:, 0], upstream[:, 1], upstream[:, 2] + tails[:, 0], upstream[:, 3] + tails[:, 1]], axis=0
    ).reshape(128, 512)
    through = upstream * slope
    cubed = scale * scale * scale
    through_mean = jnp.mean(values * through, axis=-1, keepdims=True)
    gradient = masked + scale * through - values * cubed * through_mean
    grad_ref[...] = (gradient * live).astype(BF16)
    for copy in started[-7:]:
        copy.wait_send()


def pin(value):
    return pltpu.with_memory_space_constraint(value, pltpu.HBM)


def per_device(block_input_frames, norm_gain, kernel, output_gradient, group_count, clip_starts):
    shape = block_input_frames.shape
    tables = [jnp.asarray(table(), BF16) for table in (swap_table, column_table, corner_table, edge_table)]
    vmem, smem, hbm = [pl.BlockSpec(memory_space=space) for space in (pltpu.VMEM, pltpu.SMEM, pltpu.HBM)]
    dma = pltpu.SemaphoreType.DMA
    block_out, input_grad = pl.pallas_call(
        body,
        out_shape=[jax.ShapeDtypeStruct((128, 512), BF16)] * 2,
        in_specs=[hbm] * 4 + [smem] * 2 + [hbm] * 4,
        out_specs=[vmem] * 2,
        scratch_shapes=[
            pltpu.VMEM((128, 512), BF16),
            pltpu.VMEM((1, 512), F32),
            pltpu.VMEM((27, 16, 32), BF16),
            pltpu.VMEM((128, 512), BF16),
            *[pltpu.VMEM(table.shape, BF16) for table in tables],
            pltpu.VMEM((4, 16, 112, 128), BF16),
            pltpu.VMEM((2, 4, 4, 27, 16, 128), BF16),
            pltpu.VMEM((128, 512), BF16),
            pltpu.VMEM((128, 512), BF16),
            pltpu.VMEM((2, 96, 512), BF16),
            pltpu.VMEM((2, 96, 512), BF16),
            pltpu.VMEM((2, 64, 128), BF16),
            pltpu.VMEM((2, 64, 128), BF16),
            pltpu.VMEM((4, 384, 128), BF16),
            pltpu.VMEM((4, 384, 128), BF16),
            pltpu.VMEM((4, 4, 256, 128), BF16),
            pltpu.VMEM((3, 6, 6, 32, 128), BF16),
            pltpu.VMEM((4, 3, 6, 4, 32, 128), BF16),
            pltpu.VMEM((512, 512), F32),
            pltpu.VMEM((512, 384), F32),
            pltpu.VMEM((4, 128, 512), BF16),
            pltpu.VMEM((3, 128, 512), BF16),
            pltpu.VMEM((4, 128, 128), BF16),
            pltpu.VMEM((4, 128, 128), BF16),
            pltpu.VMEM((4, 64, 128), BF16),
            pltpu.VMEM((4, 64, 128), BF16),
            dma((8,)),
            dma((8,)), dma((8,)),
            dma((1,)), dma((1,)),
            dma((2, 8)), dma((2, 8)),
            dma((2, 3)), dma((2, 3)),
            dma((2, 3, 2)), dma((2, 3, 2)),
            dma((2, 5)), dma((2, 5)),
            dma((5,)), dma((5,)),
            dma((4,)), dma((4,)),
            dma((3,)), dma((3,)),
            dma((3,)), dma((3,)),
            dma((4,)), dma((4,)),
        ],
        compiler_params=pltpu.CompilerParams(
            collective_id=0, has_side_effects=True, vmem_limit_bytes=40 * 1024 * 1024
        ),
        cost_estimate=pl.CostEstimate(flops=7_200_000_000, bytes_accessed=20_000_000, transcendentals=200_000),
    )(
        pin(block_input_frames.reshape(128, 512)),
        pin(norm_gain.reshape(1, 512)),
        pin(kernel.reshape(27, 16, 32)),
        pin(output_gradient.reshape(128, 512)),
        group_count,
        clip_starts,
        *[pin(table) for table in tables],
    )
    return block_out.reshape(shape), input_grad.reshape(shape)


def solution(mesh):
    frames = P("group", None, "tile", None, None, None)
    return jax.shard_map(
        per_device,
        mesh=mesh,
        in_specs=(frames, P(), P(None, None, None, "group", "tile"), frames, P("group"), P("group")),
        out_specs=(frames, frames),
        check_vma=False,
    )
```

```python
import numpy as np
import jax
import jax.numpy as jnp
from jax import lax
from jax.experimental import pallas as pl
from jax.experimental.pallas import tpu as pltpu
from jax.sharding import PartitionSpec as P

MESH = pl.DeviceIdType.MESH
EPSILON = 1e-06
F32, BF16 = jnp.float32, jnp.bfloat16


def swap_table():
    table = np.zeros((512, 512), np.float32)
    for a in range(4):
        for b in range(4):
            for o in range(32):
                table[a * 128 + b * 32 + o, b * 128 + a * 32 + o] = 1
    return table.reshape(512, 4, 128).transpose(1, 0, 2)


def column_table():
    table = np.zeros((32, 128), np.float32)
    for it in range(16):
        table[it, it * 8 + 7] = 1
        table[16 + it, it * 8] = 1
    return table


def corner_table():
    table = np.zeros((4, 64, 128), np.float32)
    for k in range(4):
        for corner, (i, j) in enumerate(((3, 7), (3, 0), (0, 7), (0, 0))):
            for t in range(4):
                table[k, 16 * corner + 4 * k + t, (i * 4 + t) * 8 + j] = 1
    return table


def edge_table():
    table = np.zeros((4, 64, 128), np.float32)
    for k in range(4):
        for side in range(2):
            for t in range(4):
                first = 16 * t + 8 * side
                table[k, first, 32 + 16 * side + 4 * k + t] = 1
                table[k, first + 5, 64 + 16 * side + 4 * k + t] = 1
                for i in range(4):
                    table[k, first + 1 + i, 16 * side + i * 4 + t] = 1
    return table


SHARDS = (0, -1, 7, -4, -7, 4, 1, -2, 6, -5, -8, 3, -3, -6, 5, 2)
CHUNKS = ((0, 1, 0), (1, 3, 0), (4, 3, 1), (7, 5, 0), (12, 4, 1))
STRIP_STEPS, COLUMN_STEPS, CORNER_STEPS = (4, -4), (1, -1), (5, 3, -3, -5)


def dot(left, right):
    return jnp.dot(left, right, preferred_element_type=F32)


def swap_lanes(value, swap_ref):
    return dot(value, jnp.concatenate([swap_ref[k] for k in range(4)], axis=1))


def body(
    x_hbm, gain_hbm, w_hbm, g_hbm, count_ref, starts_ref, swap_hbm, column_hbm, corner_hbm, edge_hbm,
    out_ref, grad_ref,
    xv, gainv, wv, gv, swap_ref, column_pick, corner_pick, edge_pick,
    wz, wbuf, tsend, trecv, rows_s, rows_r, corners_s, corners_r, amsg, abuf, gb, fbuf, bbuf,
    acc_f, acc_b, psend, precv, bsend, brecv, dsend, drecv,
    in_s, z_s, z_r, t_s, t_r, h_s, h_r, a_s, a_r, gy_s, gy_r,
    wx_s, wx_r, wf_s, wf_r, wc_s, wc_r, p_s, p_r, b_s, b_r, d_s, d_r,
):
    loads = [
        pltpu.make_async_copy(src, dst, in_s.at[k])
        for k, (src, dst) in enumerate(
            (
                (w_hbm, wv), (g_hbm, gv), (x_hbm, xv), (gain_hbm, gainv), (swap_hbm, swap_ref),
                (column_hbm, column_pick), (corner_hbm, corner_pick), (edge_hbm, edge_pick),
            )
        )
    ]
    for load in loads:
        load.start()

    group = lax.axis_index("group")
    z = lax.axis_index("tile")
    x, y, c = lax.div(group, 8), lax.rem(lax.div(group, 2), 4), lax.rem(group, 2)

    def device(x_at, y_at, c_at, z_at):
        return (x_at * 8 + y_at * 2 + c_at, z_at)

    def mod4(value):
        return lax.rem(value + 4, 4)

    def zmove(step):
        return (group, lax.rem(z + step + 16, 16))

    core = device(x, y, 1 - c, z)
    x_right, x_left = device(mod4(x + 1), y, c, z), device(mod4(x - 1), y, c, z)
    y_peers = [device(x, mod4(y + d), c, z) for d in (1, 2, 3)]
    y_right, y_left = y_peers[0], y_peers[2]
    following, previous = lax.rem(group + 1, 32), lax.rem(group + 31, 32)
    after, before = (following, z), (previous, z)
    head_targets = [(lax.rem(x * 8 + 2 * k + c + 31, 32), z) for k in range(4)]
    head_sources = [device(lax.div(following, 8), k, lax.rem(following, 2), z) for k in range(4)]

    barrier = pltpu.get_barrier_semaphore()
    partners = [core, x_right, x_left, *y_peers, after, before, *head_sources]
    partners += [zmove(step) for step in STRIP_STEPS + COLUMN_STEPS + CORNER_STEPS + (7, -7)]
    for partner in partners:
        pl.semaphore_signal(barrier, inc=1, device_id=partner, device_id_type=MESH)

    started = []

    def remote(src, dst, send_sem, recv_sem, target):
        return pltpu.make_async_remote_copy(
            src_ref=src, dst_ref=dst, send_sem=send_sem, recv_sem=recv_sem, device_id=target, device_id_type=MESH
        )

    def send(src, dst, send_sem, recv_sem, target):
        copy = remote(src, dst, send_sem, recv_sem, target)
        copy.start()
        started.append(copy)

    def arrived(dst, sem):
        remote(dst, dst, sem, sem, core).wait_recv()

    def z_first():
        for k, step in enumerate(SHARDS[1:7]):
            send(wz.at[x, 0], wz.at[x, 1 + k], z_s.at[k], z_r.at[k], zmove(-step))

    def z_first_wait():
        for k in range(6):
            arrived(wz.at[x, 1 + k], z_r.at[k])

    def z_second():
        send(wz.at[x, pl.ds(1, 5)], wz.at[x, pl.ds(7, 5)], z_s.at[6], z_r.at[6], zmove(1))
        send(wz.at[x, pl.ds(3, 4)], wz.at[x, pl.ds(12, 4)], z_s.at[7], z_r.at[7], zmove(-1))

    def z_second_wait():
        arrived(wz.at[x, pl.ds(7, 5)], z_r.at[6])
        arrived(wz.at[x, pl.ds(12, 4)], z_r.at[7])

    def x_block(step, k):
        return wz.at[mod4(x + step), pl.ds(CHUNKS[k][0], CHUNKS[k][1])]

    def x_send(k, side):
        block = x_block(0, k)
        send(block, block, wx_s.at[side, k], wx_r.at[side, k], x_left if side else x_right)

    def x_arrived(k, side):
        arrived(x_block(1 if side else -1, k), wx_r.at[side, k])

    def x_pass(k):
        side = CHUNKS[k][2]
        x_arrived(k, side)
        block = x_block(1 if side else -1, k)
        send(block, block, wf_s.at[k], wf_r.at[k], x_left if side else x_right)

    def x_far(k):
        arrived(x_block(2, k), wf_r.at[k])

    places = []
    for shard in range(16):
        away = lax.rem(shard - z + 24, 16) - 8
        place = jnp.int32(0)
        for slot in range(1, 16):
            place = jnp.where(away == SHARDS[slot], slot, place)
        places.append(place)

    def w_layout(step):
        at = mod4(x + step)
        rows = []
        for quad in range(4):
            rows.append(jnp.concatenate([wz[at, places[quad * 4 + j]] for j in range(4)], axis=1))
        full = swap_lanes(jnp.concatenate(rows, axis=0), swap_ref).astype(BF16)
        for quad in range(4):
            for tap in range(27):
                row, lanes = quad * 112 + (tap // 4) * 16, (tap % 4) * 128
                wbuf[c, at, quad, tap] = full[row : row + 16, lanes : lanes + 128]
        whole = wbuf.at[c, at]
        send(whole, whole, wc_s.at[step + 1], wc_r.at[step + 1], core)

    def w_core():
        for step in (0, -1, 1, 2):
            arrived(wbuf.at[1 - c, mod4(x + step)], wc_r.at[step + 1])

    def y_block(owner, half, part):
        return gb.at[owner, pl.ds(2 * half, 2), pl.ds(128 * part, 128)]

    def y_start(part):
        for half in range(2):
            block = y_block(y, half, part)
            send(block, block, gy_s.at[part, 0, half], gy_r.at[part, 0, half], y_right)
            send(block, block, gy_s.at[part, 1, half], gy_r.at[part, 1, half], y_left)

    def y_relay(part):
        for side, step, target in ((0, -1, y_right), (1, 1, y_left)):
            for half in (side, 1 - side):
                block = y_block(mod4(y + step), half, part)
                arrived(block, gy_r.at[part, side, half])
                if half == side:
                    send(block, block, gy_s.at[part, 2, half], gy_r.at[part, 2, half], target)

    def y_far(part):
        for half in range(2):
            arrived(y_block(mod4(y + 2), half, part), gy_r.at[part, 2, half])

    def strips_start(field, tile):
        rows_s[field, 0:32] = tile[96:128]
        rows_s[field, 32:64] = tile[0:32]
        for k, step in enumerate(STRIP_STEPS):
            block = pl.ds(32 * k, 32)
            send(rows_s.at[field, block], rows_r.at[field, block], h_s.at[field, k], h_r.at[field, k], zmove(step))

    def columns_start(field, tile):
        rows_s[field, 64:96] = dot(column_pick[...], tile).astype(BF16)
        for k, step in enumerate(COLUMN_STEPS):
            block = pl.ds(64 + 16 * k, 16)
            send(rows_s.at[field, block], rows_r.at[field, block], h_s.at[field, 2 + k], h_r.at[field, 2 + k], zmove(step))
        corners = [dot(corner_pick[k], tile[:, k * 128 : (k + 1) * 128]) for k in range(4)]
        corners_s[field] = (corners[0] + corners[1] + corners[2] + corners[3]).astype(BF16)
        for k, step in enumerate(CORNER_STEPS):
            block = pl.ds(16 * k, 16)
            send(corners_s.at[field, block], corners_r.at[field, block], h_s.at[field, 4 + k], h_r.at[field, 4 + k], zmove(step))

    tile_row, tile_column = lax.div(z, 4), lax.rem(z, 4)

    def unless(hit):
        return jnp.where(hit, 0.0, 1.0).astype(F32)

    at_top, at_bottom = unless(tile_row == 0), unless(tile_row == 3)
    at_left, at_right = unless(tile_column == 0), unless(tile_column == 3)

    def halo_finish(field):
        for k in range(2):
            arrived(rows_r.at[field, pl.ds(32 * k, 32)], h_r.at[field, k])
        for k in range(2):
            arrived(rows_r.at[field, pl.ds(64 + 16 * k, 16)], h_r.at[field, 2 + k])
        for k in range(4):
            arrived(corners_r.at[field, pl.ds(16 * k, 16)], h_r.at[field, 4 + k])
        above = rows_r[field, 0:32].astype(F32) * at_top
        below = rows_r[field, 32:64].astype(F32) * at_bottom
        row_at = lax.broadcasted_iota(jnp.int32, (64, 128), 0)
        keep = jnp.where((row_at & 8) == 0, at_left, at_right)
        keep = keep * jnp.where((row_at & 7) == 0, at_top, 1.0) * jnp.where((row_at & 7) == 5, at_bottom, 1.0)
        flag = jnp.where(row_at == 6, source, 0.0)
        edges = []
        for k in range(4):
            picks = jnp.concatenate([rows_r[field, 64:96, k * 128 : (k + 1) * 128], corners_r[field]], axis=0)
            edges.append(dot(edge_pick[k, :, 0:96], picks) * keep + flag)
        return jnp.concatenate([above, below, jnp.concatenate(edges, axis=1)], axis=0).astype(BF16)

    loads[0].wait()
    packed = jnp.zeros((112, 128), F32)
    for k in range(4):
        taps = [wv[4 * row + k] if 4 * row + k < 27 else jnp.zeros((16, 32), BF16) for row in range(7)]
        lane_at = lax.broadcasted_iota(jnp.int32, (32, 128), 1) - lax.broadcasted_iota(jnp.int32, (32, 128), 0)
        packed = packed + dot(jnp.concatenate(taps, axis=0), jnp.where(lane_at == 32 * k, 1.0, 0.0).astype(BF16))
    wz[x, 0] = packed.astype(BF16)

    live = jnp.where(count_ref[0] > 0, 1.0, 0.0).astype(F32)
    fresh = jnp.where(starts_ref[0] == 0, 1.0, 0.0).astype(F32)
    source = live * fresh * jnp.where(group > 0, 1.0, 0.0).astype(F32)

    def swap_frames(value):
        value = value.reshape(4, 4, 8, value.shape[1])
        return jnp.concatenate([value[:, k] for k in range(4)], axis=0).reshape(128, value.shape[3])

    loads[1].wait()
    masked = gv[...].astype(F32) * live
    grad_tile = swap_frames(masked).astype(BF16)
    for k in range(4):
        gb[y, k, 0:128] = grad_tile[:, k * 128 : (k + 1) * 128]

    pl.semaphore_wait(barrier, len(partners))
    z_first()
    x_send(0, 0)
    x_send(0, 1)
    y_start(0)

    loads[2].wait()
    loads[3].wait()
    loads[4].wait()
    gain = gainv[...]
    values = xv[...].astype(F32)
    scale = lax.rsqrt(jnp.mean(values * values, axis=-1, keepdims=True) + EPSILON)
    normed = values * scale * gain
    activated = (normed * jax.nn.sigmoid(normed)).astype(BF16)
    swapped = swap_lanes(activated, swap_ref)
    tsend[0:64] = swapped[64:128].astype(BF16)
    act_tile = swap_frames(swapped).astype(BF16)

    def a_rows(part):
        return pl.ds(0, 128) if part == 0 else pl.ds(128, 256)

    def a_start(part, value):
        first = 0 if part == 0 else 128
        for k in range(4):
            amsg[k, first : first + value.shape[0]] = value[:, k * 128 : (k + 1) * 128]
        for d in (1, 2, 3):
            src, dst = amsg.at[mod4(y + d), a_rows(part)], abuf.at[y, a_rows(part)]
            send(src, dst, a_s.at[part, d - 1], a_r.at[part, d - 1], y_peers[d - 1])
        abuf[y, first : first + value.shape[0]] = amsg[y, first : first + value.shape[0]]

    def a_wait(part):
        for d in (1, 2, 3):
            arrived(abuf.at[mod4(y - d), a_rows(part)], a_r.at[part, d - 1])

    a_start(0, act_tile)
    for load in loads[5:]:
        load.wait()
    strips_start(0, act_tile)
    columns_start(0, act_tile)
    z_first_wait()
    z_second()
    for k, side in ((1, 0), (2, 1), (2, 0), (1, 1)):
        x_send(k, side)
    strips_start(1, grad_tile)
    columns_start(1, grad_tile)
    x_pass(0)
    y_relay(0)
    halo = halo_finish(0)
    tsend[64:80] = halo[16:32]
    tsend[80:96] = halo[48:64]
    tsend[96:128] = halo[96:128]
    send(tsend, trecv, t_s.at[0], t_r.at[0], after)
    z_second_wait()
    for k, side in ((3, 0), (4, 1), (4, 0), (3, 1)):
        x_send(k, side)
    grad_halo = halo_finish(1)
    for k in range(4):
        gb[y, k, 128:256] = grad_halo[:, k * 128 : (k + 1) * 128]
    y_start(1)
    x_pass(1)
    x_pass(2)
    w_layout(0)
    arrived(trecv, t_r.at[0])
    a_start(1, jnp.concatenate([halo, (trecv[...].astype(F32) * source).astype(BF16)], axis=0))
    x_pass(3)
    x_pass(4)
    y_relay(1)
    for k in range(5):
        x_arrived(k, 1 - CHUNKS[k][2])
    w_layout(-1)
    w_layout(1)

    def shifted(slabs, centers, edges):
        center = jnp.concatenate([slabs[k : k + 1] for k in centers], axis=0)
        sides = []
        for side in range(2):
            rows = [jnp.broadcast_to(slabs[k + side, i : i + 1], slabs.shape[1:])[None] for k, i in edges]
            sides.append(jnp.concatenate(rows, axis=0))
        at = lax.broadcasted_iota(jnp.int32, center.shape, 1)
        from_left = jnp.where(at == 0, sides[0], pltpu.roll(center, 1, 1))
        from_right = jnp.where(at == 7, sides[1], pltpu.roll(center, 7, 1))
        return from_left, center, from_right

    def own_slab(i, t):
        return 16 + t if i == 0 else 20 + t if i == 5 else (i - 1) * 4 + t

    def carried_slab(i, t):
        return 40 + t if i == 0 else 42 + t if i == 5 else 32 + t * 4 + i - 1

    grad_centers = [own_slab(i, t) for i in range(6) for t in range(4)]
    grad_edges = [(24 + 2 * t, i) for i in range(6) for t in range(4)]
    act_centers = [carried_slab(i, t) if t < 2 else own_slab(i, t - 2) for i in range(6) for t in range(6)]
    act_edges = [(44 + 2 * t, i) if t < 2 else (24 + 2 * (t - 2), i) for i in range(6) for t in range(6)]

    a_wait(0)
    a_wait(1)

    def build_f(pair, carry):
        parts = []
        for k in range(2):
            slabs = abuf[2 * pair + k].astype(F32).reshape(48, 8, 128)
            parts.append(shifted(slabs, act_centers, act_edges))
        rows = pl.ds(pl.multiple_of(16 * pair, 16), 16)
        for e in range(3):
            value = jnp.concatenate([part[e] for part in parts], axis=1).astype(BF16)
            fbuf[e, :, :, rows] = value.reshape(6, 6, 16, 128)
        return carry

    lax.fori_loop(0, 2, build_f, 0)

    def build_g(k, carry):
        half, pair = lax.div(k, 2), lax.rem(k, 2)
        parts = []
        for n in range(2):
            message = jnp.concatenate([gb[2 * pair + n, 2 * half + m] for m in range(2)], axis=1)
            parts.append(shifted(message.astype(F32).reshape(32, 8, 256), grad_centers, grad_edges))
        rows = pl.ds(pl.multiple_of(16 * pair, 16), 16)
        for e in range(3):
            value = jnp.concatenate([part[e] for part in parts], axis=1).astype(BF16)
            for m in range(2):
                bbuf[2 * half + m, e, :, :, rows] = value[:, :, m * 128 : (m + 1) * 128].reshape(6, 4, 16, 128)
        return carry

    def taps_of(r, tap):
        return jnp.concatenate([wbuf[k, i, r, tap] for i in range(4) for k in range(2)], axis=0)

    def forward(pair):
        acc_f[...] = jnp.zeros_like(acc_f)

        def frame_tap(a, carry):
            windows, taps = [], []
            for b in range(3):
                for e in range(3):
                    windows.append(fbuf[e, b : b + 4, pl.ds(a, 4)].reshape(512, 128))
                    tap = a * 9 + b * 3 + e
                    taps.append(jnp.concatenate([taps_of(2 * pair + k, tap) for k in range(2)], axis=1))
            acc_f[...] += dot(jnp.concatenate(windows, axis=1), jnp.concatenate(taps, axis=0))
            return carry

        lax.fori_loop(0, 3, frame_tap, 0)
        total = acc_f[...].reshape(16, 32, 256)
        for other in range(4):
            psend[pair, other] = total[:, other * 8 : other * 8 + 8].reshape(128, 256).astype(BF16)
        for d in (1, 2, 3):
            src, dst = psend.at[pair, mod4(y + d)], precv.at[pair, d - 1]
            send(src, dst, p_s.at[pair, d - 1], p_r.at[pair, d - 1], y_peers[d - 1])

    def backward():
        acc_b[...] = jnp.zeros_like(acc_b)

        def row_tap(b, carry):
            windows, taps = [], []
            for e in range(3):
                for quad in range(4):
                    windows.append(bbuf[quad, 2 - e, pl.ds(2 - b, 4)].reshape(512, 128))
                    taps.append(jnp.concatenate([taps_of(quad, a * 9 + b * 3 + e) for a in range(3)], axis=0))
            acc_b[...] += lax.dot_general(
                jnp.concatenate(windows, axis=1),
                jnp.concatenate(taps, axis=1),
                (((1,), (1,)), ((), ())),
                preferred_element_type=F32,
            )
            return carry

        lax.fori_loop(0, 3, row_tap, 0)

    sigma = jax.nn.sigmoid(normed)
    slope = sigma * (1.0 + normed * (1.0 - sigma)) * gain
    for k in range(5):
        x_far(k)
    w_layout(2)
    y_far(0)
    y_far(1)
    lax.fori_loop(0, 4, build_g, 0)
    w_core()
    forward(0)
    forward(1)
    backward()
    taps = acc_b[...].reshape(4, 4, 32, 384)
    spread = []
    for u in range(6):
        terms = [taps[:, u - a, :, a * 128 : (a + 1) * 128] for a in range(3) if 0 <= u - a < 4]
        spread.append(sum(terms[1:], terms[0]))
    for other in range(4):
        slots = [part[:, other * 8 : other * 8 + 8] for part in spread]
        bsend[other] = jnp.stack(slots[2:], axis=1).reshape(128, 128).astype(BF16)
        flag = gb[other, 0, 192:208].astype(F32)[6:7]
        dsend[other] = (jnp.stack(slots[:2], axis=1).reshape(64, 128) * flag).astype(BF16)
    for d in (1, 2, 3):
        send(bsend.at[mod4(y + d)], brecv.at[y], b_s.at[d - 1], b_r.at[d - 1], y_peers[d - 1])
    for k in range(4):
        send(dsend.at[k], drecv.at[y], d_s.at[k], d_r.at[y], head_targets[k])
    brecv[y] = bsend[y]
    halves = []
    for pair in range(2):
        total = psend[pair, y].astype(F32)
        for d in (1, 2, 3):
            arrived(precv.at[pair, d - 1], p_r.at[pair, d - 1])
            total = total + precv[pair, d - 1].astype(F32)
        halves.append(total)
    mixed = jnp.concatenate(halves, axis=1)
    out_ref[...] = ((values + swap_frames(mixed)) * live).astype(BF16)
    for copy in started[:-7]:
        copy.wait_send()
    for d in (1, 2, 3):
        arrived(brecv.at[mod4(y - d)], b_r.at[d - 1])
    for k in range(4):
        arrived(drecv.at[k], d_r.at[k])
    own = jnp.concatenate([brecv[k] for k in range(4)], axis=1).astype(F32).reshape(4, 4, 8, 512)
    heads = jnp.concatenate([drecv[k] for k in range(4)], axis=1).astype(F32).reshape(4, 2, 8, 512)
    upstream = swap_lanes(own.reshape(128, 512).astype(BF16), swap_ref).reshape(4, 4, 8, 512)
    tails = swap_lanes(heads.reshape(64, 512).astype(BF16), swap_ref).reshape(4, 2, 8, 512)
    upstream = jnp.concatenate(
        [upstream[:, 0], upstream[:, 1], upstream[:, 2] + tails[:, 0], upstream[:, 3] + tails[:, 1]], axis=0
    ).reshape(128, 512)
    through = upstream * slope
    cubed = scale * scale * scale
    through_mean = jnp.mean(values * through, axis=-1, keepdims=True)
    gradient = masked + scale * through - values * cubed * through_mean
    grad_ref[...] = (gradient * live).astype(BF16)
    for copy in started[-7:]:
        copy.wait_send()


def pin(value):
    return pltpu.with_memory_space_constraint(value, pltpu.HBM)


def per_device(block_input_frames, norm_gain, kernel, output_gradient, group_count, clip_starts):
    shape = block_input_frames.shape
    tables = [jnp.asarray(table(), BF16) for table in (swap_table, column_table, corner_table, edge_table)]
    vmem, smem, hbm = [pl.BlockSpec(memory_space=space) for space in (pltpu.VMEM, pltpu.SMEM, pltpu.HBM)]
    dma = pltpu.SemaphoreType.DMA
    block_out, input_grad = pl.pallas_call(
        body,
        out_shape=[jax.ShapeDtypeStruct((128, 512), BF16)] * 2,
        in_specs=[hbm] * 4 + [smem] * 2 + [hbm] * 4,
        out_specs=[vmem] * 2,
        scratch_shapes=[
            pltpu.VMEM((128, 512), BF16),
            pltpu.VMEM((1, 512), F32),
            pltpu.VMEM((27, 16, 32), BF16),
            pltpu.VMEM((128, 512), BF16),
            *[pltpu.VMEM(table.shape, BF16) for table in tables],
            pltpu.VMEM((4, 16, 112, 128), BF16),
            pltpu.VMEM((2, 4, 4, 27, 16, 128), BF16),
            pltpu.VMEM((128, 512), BF16),
            pltpu.VMEM((128, 512), BF16),
            pltpu.VMEM((2, 96, 512), BF16),
            pltpu.VMEM((2, 96, 512), BF16),
            pltpu.VMEM((2, 64, 128), BF16),
            pltpu.VMEM((2, 64, 128), BF16),
            pltpu.VMEM((4, 384, 128), BF16),
            pltpu.VMEM((4, 384, 128), BF16),
            pltpu.VMEM((4, 4, 256, 128), BF16),
            pltpu.VMEM((3, 6, 6, 32, 128), BF16),
            pltpu.VMEM((4, 3, 6, 4, 32, 128), BF16),
            pltpu.VMEM((512, 256), F32),
            pltpu.VMEM((512, 384), F32),
            pltpu.VMEM((2, 4, 128, 256), BF16),
            pltpu.VMEM((2, 3, 128, 256), BF16),
            pltpu.VMEM((4, 128, 128), BF16),
            pltpu.VMEM((4, 128, 128), BF16),
            pltpu.VMEM((4, 64, 128), BF16),
            pltpu.VMEM((4, 64, 128), BF16),
            dma((8,)),
            dma((8,)), dma((8,)),
            dma((1,)), dma((1,)),
            dma((2, 8)), dma((2, 8)),
            dma((2, 3)), dma((2, 3)),
            dma((2, 3, 2)), dma((2, 3, 2)),
            dma((2, 5)), dma((2, 5)),
            dma((5,)), dma((5,)),
            dma((4,)), dma((4,)),
            dma((2, 3)), dma((2, 3)),
            dma((3,)), dma((3,)),
            dma((4,)), dma((4,)),
        ],
        compiler_params=pltpu.CompilerParams(
            collective_id=0, has_side_effects=True, vmem_limit_bytes=40 * 1024 * 1024
        ),
        cost_estimate=pl.CostEstimate(flops=7_200_000_000, bytes_accessed=20_000_000, transcendentals=200_000),
    )(
        pin(block_input_frames.reshape(128, 512)),
        pin(norm_gain.reshape(1, 512)),
        pin(kernel.reshape(27, 16, 32)),
        pin(output_gradient.reshape(128, 512)),
        group_count,
        clip_starts,
        *[pin(table) for table in tables],
    )
    return block_out.reshape(shape), input_grad.reshape(shape)


def solution(mesh):
    frames = P("group", None, "tile", None, None, None)
    return jax.shard_map(
        per_device,
        mesh=mesh,
        in_specs=(frames, P(), P(None, None, None, "group", "tile"), frames, P("group"), P("group")),
        out_specs=(frames, frames),
        check_vma=False,
    )
```

```python
import numpy as np
import jax
import jax.numpy as jnp
from jax import lax
from jax.experimental import pallas as pl
from jax.experimental.pallas import tpu as pltpu
from jax.sharding import PartitionSpec as P

MESH = pl.DeviceIdType.MESH
EPSILON = 1e-06
F32, BF16 = jnp.float32, jnp.bfloat16


def swap_table():
    table = np.zeros((512, 512), np.float32)
    for a in range(4):
        for b in range(4):
            for o in range(32):
                table[a * 128 + b * 32 + o, b * 128 + a * 32 + o] = 1
    return table.reshape(512, 4, 128).transpose(1, 0, 2)


def column_table():
    table = np.zeros((32, 128), np.float32)
    for it in range(16):
        table[it, it * 8 + 7] = 1
        table[16 + it, it * 8] = 1
    return table


def corner_table():
    table = np.zeros((4, 64, 128), np.float32)
    for k in range(4):
        for corner, (i, j) in enumerate(((3, 7), (3, 0), (0, 7), (0, 0))):
            for t in range(4):
                table[k, 16 * corner + 4 * k + t, (i * 4 + t) * 8 + j] = 1
    return table


def edge_table():
    table = np.zeros((4, 64, 128), np.float32)
    for k in range(4):
        for side in range(2):
            for t in range(4):
                first = 16 * t + 8 * side
                table[k, first, 32 + 16 * side + 4 * k + t] = 1
                table[k, first + 5, 64 + 16 * side + 4 * k + t] = 1
                for i in range(4):
                    table[k, first + 1 + i, 16 * side + i * 4 + t] = 1
    return table


SHARDS = (0, -1, 6, -6, 1, -2, 5, -7, 7, -5, 2, -3, 4, -8, -4, 3)
CHUNKS = ((0, 1, 0), (1, 2, 0), (3, 2, 1), (5, 3, 0), (8, 3, 1), (11, 3, 0), (14, 2, 1))
STRIP_STEPS, COLUMN_STEPS, CORNER_STEPS = (4, -4), (1, -1), (5, 3, -3, -5)


def dot(left, right):
    return jnp.dot(left, right, preferred_element_type=F32)


def swap_lanes(value, swap_ref):
    return dot(value, jnp.concatenate([swap_ref[k] for k in range(4)], axis=1))


def body(
    x_hbm, gain_hbm, w_hbm, g_hbm, count_ref, starts_ref, swap_hbm, column_hbm, corner_hbm, edge_hbm,
    out_ref, grad_ref,
    xv, gainv, wv, gv, swap_ref, column_pick, corner_pick, edge_pick,
    wz, wbuf, tsend, trecv, rows_s, rows_r, corners_s, corners_r, amsg, abuf, gb, fbuf, bbuf,
    acc_f, acc_b, psend, precv, bsend, brecv, dsend, drecv,
    in_s, z_s, z_r, t_s, t_r, h_s, h_r, a_s, a_r, gy_s, gy_r,
    wx_s, wx_r, wf_s, wf_r, wc_s, wc_r, p_s, p_r, b_s, b_r, d_s, d_r,
):
    loads = [
        pltpu.make_async_copy(src, dst, in_s.at[k])
        for k, (src, dst) in enumerate(
            (
                (w_hbm, wv), (g_hbm, gv), (x_hbm, xv), (gain_hbm, gainv), (swap_hbm, swap_ref),
                (column_hbm, column_pick), (corner_hbm, corner_pick), (edge_hbm, edge_pick),
            )
        )
    ]
    for load in loads:
        load.start()

    group = lax.axis_index("group")
    z = lax.axis_index("tile")
    x, y, c = lax.div(group, 8), lax.rem(lax.div(group, 2), 4), lax.rem(group, 2)

    def device(x_at, y_at, c_at, z_at):
        return (x_at * 8 + y_at * 2 + c_at, z_at)

    def mod4(value):
        return lax.rem(value + 4, 4)

    def zmove(step):
        return (group, lax.rem(z + step + 16, 16))

    core = device(x, y, 1 - c, z)
    x_right, x_left = device(mod4(x + 1), y, c, z), device(mod4(x - 1), y, c, z)
    y_peers = [device(x, mod4(y + d), c, z) for d in (1, 2, 3)]
    y_right, y_left = y_peers[0], y_peers[2]
    following, previous = lax.rem(group + 1, 32), lax.rem(group + 31, 32)
    after, before = (following, z), (previous, z)
    head_targets = [(lax.rem(x * 8 + 2 * k + c + 31, 32), z) for k in range(4)]
    head_sources = [device(lax.div(following, 8), k, lax.rem(following, 2), z) for k in range(4)]

    barrier = pltpu.get_barrier_semaphore()
    partners = [core, x_right, x_left, *y_peers, after, before, *head_sources]
    partners += [zmove(step) for step in STRIP_STEPS + COLUMN_STEPS + CORNER_STEPS + (6, -6)]
    for partner in partners:
        pl.semaphore_signal(barrier, inc=1, device_id=partner, device_id_type=MESH)

    started = []

    def remote(src, dst, send_sem, recv_sem, target):
        return pltpu.make_async_remote_copy(
            src_ref=src, dst_ref=dst, send_sem=send_sem, recv_sem=recv_sem, device_id=target, device_id_type=MESH
        )

    def send(src, dst, send_sem, recv_sem, target):
        copy = remote(src, dst, send_sem, recv_sem, target)
        copy.start()
        started.append(copy)

    def arrived(dst, sem):
        remote(dst, dst, sem, sem, core).wait_recv()

    def z_first():
        for k, step in enumerate(SHARDS[1:5]):
            send(wz.at[x, 0], wz.at[x, 1 + k], z_s.at[k], z_r.at[k], zmove(-step))

    def z_first_wait():
        for k in range(4):
            arrived(wz.at[x, 1 + k], z_r.at[k])

    def z_second():
        send(wz.at[x, pl.ds(1, 3)], wz.at[x, pl.ds(5, 3)], z_s.at[4], z_r.at[4], zmove(1))
        send(wz.at[x, pl.ds(2, 3)], wz.at[x, pl.ds(8, 3)], z_s.at[5], z_r.at[5], zmove(-1))

    def z_second_wait():
        arrived(wz.at[x, pl.ds(5, 3)], z_r.at[4])
        arrived(wz.at[x, pl.ds(8, 3)], z_r.at[5])

    def z_third():
        send(wz.at[x, pl.ds(5, 3)], wz.at[x, pl.ds(11, 3)], z_s.at[6], z_r.at[6], zmove(1))
        send(wz.at[x, pl.ds(9, 2)], wz.at[x, pl.ds(14, 2)], z_s.at[7], z_r.at[7], zmove(-1))

    def z_third_wait():
        arrived(wz.at[x, pl.ds(11, 3)], z_r.at[6])
        arrived(wz.at[x, pl.ds(14, 2)], z_r.at[7])

    def x_block(step, k):
        return wz.at[mod4(x + step), pl.ds(CHUNKS[k][0], CHUNKS[k][1])]

    def x_send(k, side):
        block = x_block(0, k)
        send(block, block, wx_s.at[side, k], wx_r.at[side, k], x_left if side else x_right)

    def x_arrived(k, side):
        arrived(x_block(1 if side else -1, k), wx_r.at[side, k])

    def x_pass(k):
        side = CHUNKS[k][2]
        x_arrived(k, side)
        block = x_block(1 if side else -1, k)
        send(block, block, wf_s.at[k], wf_r.at[k], x_left if side else x_right)

    def x_far(k):
        arrived(x_block(2, k), wf_r.at[k])

    places = []
    for shard in range(16):
        away = lax.rem(shard - z + 24, 16) - 8
        place = jnp.int32(0)
        for slot in range(1, 16):
            place = jnp.where(away == SHARDS[slot], slot, place)
        places.append(place)

    def w_layout(step):
        at = mod4(x + step)
        rows = []
        for quad in range(4):
            rows.append(jnp.concatenate([wz[at, places[quad * 4 + j]] for j in range(4)], axis=1))
        full = swap_lanes(jnp.concatenate(rows, axis=0), swap_ref).astype(BF16)
        for quad in range(4):
            for tap in range(27):
                row, lanes = quad * 112 + (tap // 4) * 16, (tap % 4) * 128
                wbuf[c, at, quad, tap] = full[row : row + 16, lanes : lanes + 128]
        whole = wbuf.at[c, at]
        send(whole, whole, wc_s.at[step + 1], wc_r.at[step + 1], core)

    def w_core():
        for step in (0, -1, 1, 2):
            arrived(wbuf.at[1 - c, mod4(x + step)], wc_r.at[step + 1])

    def y_block(owner, half, part):
        return gb.at[owner, pl.ds(2 * half, 2), pl.ds(128 * part, 128)]

    def y_start(part):
        for half in range(2):
            block = y_block(y, half, part)
            send(block, block, gy_s.at[part, 0, half], gy_r.at[part, 0, half], y_right)
            send(block, block, gy_s.at[part, 1, half], gy_r.at[part, 1, half], y_left)

    def y_relay(part):
        for side, step, target in ((0, -1, y_right), (1, 1, y_left)):
            for half in (side, 1 - side):
                block = y_block(mod4(y + step), half, part)
                arrived(block, gy_r.at[part, side, half])
                if half == side:
                    send(block, block, gy_s.at[part, 2, half], gy_r.at[part, 2, half], target)

    def y_far(part):
        for half in range(2):
            arrived(y_block(mod4(y + 2), half, part), gy_r.at[part, 2, half])

    def strips_start(field, tile):
        rows_s[field, 0:32] = tile[96:128]
        rows_s[field, 32:64] = tile[0:32]
        for k, step in enumerate(STRIP_STEPS):
            block = pl.ds(32 * k, 32)
            send(rows_s.at[field, block], rows_r.at[field, block], h_s.at[field, k], h_r.at[field, k], zmove(step))

    def columns_start(field, tile):
        rows_s[field, 64:96] = dot(column_pick[...], tile).astype(BF16)
        for k, step in enumerate(COLUMN_STEPS):
            block = pl.ds(64 + 16 * k, 16)
            send(rows_s.at[field, block], rows_r.at[field, block], h_s.at[field, 2 + k], h_r.at[field, 2 + k], zmove(step))
        corners = [dot(corner_pick[k], tile[:, k * 128 : (k + 1) * 128]) for k in range(4)]
        corners_s[field] = (corners[0] + corners[1] + corners[2] + corners[3]).astype(BF16)
        for k, step in enumerate(CORNER_STEPS):
            block = pl.ds(16 * k, 16)
            send(corners_s.at[field, block], corners_r.at[field, block], h_s.at[field, 4 + k], h_r.at[field, 4 + k], zmove(step))

    tile_row, tile_column = lax.div(z, 4), lax.rem(z, 4)

    def unless(hit):
        return jnp.where(hit, 0.0, 1.0).astype(F32)

    at_top, at_bottom = unless(tile_row == 0), unless(tile_row == 3)
    at_left, at_right = unless(tile_column == 0), unless(tile_column == 3)

    def halo_finish(field):
        for k in range(2):
            arrived(rows_r.at[field, pl.ds(32 * k, 32)], h_r.at[field, k])
        for k in range(2):
            arrived(rows_r.at[field, pl.ds(64 + 16 * k, 16)], h_r.at[field, 2 + k])
        for k in range(4):
            arrived(corners_r.at[field, pl.ds(16 * k, 16)], h_r.at[field, 4 + k])
        above = rows_r[field, 0:32].astype(F32) * at_top
        below = rows_r[field, 32:64].astype(F32) * at_bottom
        row_at = lax.broadcasted_iota(jnp.int32, (64, 128), 0)
        keep = jnp.where((row_at & 8) == 0, at_left, at_right)
        keep = keep * jnp.where((row_at & 7) == 0, at_top, 1.0) * jnp.where((row_at & 7) == 5, at_bottom, 1.0)
        flag = jnp.where(row_at == 6, source, 0.0)
        edges = []
        for k in range(4):
            picks = jnp.concatenate([rows_r[field, 64:96, k * 128 : (k + 1) * 128], corners_r[field]], axis=0)
            edges.append(dot(edge_pick[k, :, 0:96], picks) * keep + flag)
        return jnp.concatenate([above, below, jnp.concatenate(edges, axis=1)], axis=0).astype(BF16)

    loads[0].wait()
    packed = jnp.zeros((112, 128), F32)
    for k in range(4):
        taps = [wv[4 * row + k] if 4 * row + k < 27 else jnp.zeros((16, 32), BF16) for row in range(7)]
        lane_at = lax.broadcasted_iota(jnp.int32, (32, 128), 1) - lax.broadcasted_iota(jnp.int32, (32, 128), 0)
        packed = packed + dot(jnp.concatenate(taps, axis=0), jnp.where(lane_at == 32 * k, 1.0, 0.0).astype(BF16))
    wz[x, 0] = packed.astype(BF16)

    live = jnp.where(count_ref[0] > 0, 1.0, 0.0).astype(F32)
    fresh = jnp.where(starts_ref[0] == 0, 1.0, 0.0).astype(F32)
    source = live * fresh * jnp.where(group > 0, 1.0, 0.0).astype(F32)

    def swap_frames(value):
        value = value.reshape(4, 4, 8, value.shape[1])
        return jnp.concatenate([value[:, k] for k in range(4)], axis=0).reshape(128, value.shape[3])

    loads[1].wait()
    masked = gv[...].astype(F32) * live
    grad_tile = swap_frames(masked).astype(BF16)
    for k in range(4):
        gb[y, k, 0:128] = grad_tile[:, k * 128 : (k + 1) * 128]

    pl.semaphore_wait(barrier, len(partners))
    z_first()
    x_send(0, 0)
    x_send(0, 1)
    y_start(0)

    loads[2].wait()
    loads[3].wait()
    loads[4].wait()
    gain = gainv[...]
    values = xv[...].astype(F32)
    scale = lax.rsqrt(jnp.mean(values * values, axis=-1, keepdims=True) + EPSILON)
    normed = values * scale * gain
    activated = (normed * jax.nn.sigmoid(normed)).astype(BF16)
    swapped = swap_lanes(activated, swap_ref)
    tsend[0:64] = swapped[64:128].astype(BF16)
    act_tile = swap_frames(swapped).astype(BF16)

    def a_rows(part):
        return pl.ds(0, 128) if part == 0 else pl.ds(128, 256)

    def a_start(part, value):
        first = 0 if part == 0 else 128
        for k in range(4):
            amsg[k, first : first + value.shape[0]] = value[:, k * 128 : (k + 1) * 128]
        for d in (1, 2, 3):
            src, dst = amsg.at[mod4(y + d), a_rows(part)], abuf.at[y, a_rows(part)]
            send(src, dst, a_s.at[part, d - 1], a_r.at[part, d - 1], y_peers[d - 1])
        abuf[y, first : first + value.shape[0]] = amsg[y, first : first + value.shape[0]]

    def a_wait(part):
        for d in (1, 2, 3):
            arrived(abuf.at[mod4(y - d), a_rows(part)], a_r.at[part, d - 1])

    a_start(0, act_tile)
    for load in loads[5:]:
        load.wait()
    strips_start(0, act_tile)
    columns_start(0, act_tile)
    z_first_wait()
    z_second()
    for k, side in ((1, 0), (2, 1), (2, 0), (1, 1)):
        x_send(k, side)
    strips_start(1, grad_tile)
    columns_start(1, grad_tile)
    x_pass(0)
    y_relay(0)
    halo = halo_finish(0)
    tsend[64:80] = halo[16:32]
    tsend[80:96] = halo[48:64]
    tsend[96:128] = halo[96:128]
    send(tsend, trecv, t_s.at[0], t_r.at[0], after)
    z_second_wait()
    z_third()
    for k, side in ((3, 0), (4, 1), (4, 0), (3, 1)):
        x_send(k, side)
    x_pass(1)
    x_pass(2)
    grad_halo = halo_finish(1)
    for k in range(4):
        gb[y, k, 128:256] = grad_halo[:, k * 128 : (k + 1) * 128]
    y_start(1)
    z_third_wait()
    for k, side in ((5, 0), (6, 1), (6, 0), (5, 1)):
        x_send(k, side)
    x_pass(3)
    x_pass(4)
    w_layout(0)
    arrived(trecv, t_r.at[0])
    a_start(1, jnp.concatenate([halo, (trecv[...].astype(F32) * source).astype(BF16)], axis=0))
    x_pass(5)
    x_pass(6)
    y_relay(1)
    for k in range(7):
        x_arrived(k, 1 - CHUNKS[k][2])
    w_layout(-1)
    w_layout(1)

    def shifted(slabs, centers, edges):
        center = jnp.concatenate([slabs[k : k + 1] for k in centers], axis=0)
        sides = []
        for side in range(2):
            rows = [jnp.broadcast_to(slabs[k + side, i : i + 1], slabs.shape[1:])[None] for k, i in edges]
            sides.append(jnp.concatenate(rows, axis=0))
        at = lax.broadcasted_iota(jnp.int32, center.shape, 1)
        from_left = jnp.where(at == 0, sides[0], pltpu.roll(center, 1, 1))
        from_right = jnp.where(at == 7, sides[1], pltpu.roll(center, 7, 1))
        return from_left, center, from_right

    def own_slab(i, t):
        return 16 + t if i == 0 else 20 + t if i == 5 else (i - 1) * 4 + t

    def carried_slab(i, t):
        return 40 + t if i == 0 else 42 + t if i == 5 else 32 + t * 4 + i - 1

    grad_centers = [own_slab(i, t) for i in range(6) for t in range(4)]
    grad_edges = [(24 + 2 * t, i) for i in range(6) for t in range(4)]
    act_centers = [carried_slab(i, t) if t < 2 else own_slab(i, t - 2) for i in range(6) for t in range(6)]
    act_edges = [(44 + 2 * t, i) if t < 2 else (24 + 2 * (t - 2), i) for i in range(6) for t in range(6)]

    a_wait(0)
    a_wait(1)

    def build_f(pair, carry):
        parts = []
        for k in range(2):
            slabs = abuf[2 * pair + k].astype(F32).reshape(48, 8, 128)
            parts.append(shifted(slabs, act_centers, act_edges))
        rows = pl.ds(pl.multiple_of(16 * pair, 16), 16)
        for e in range(3):
            value = jnp.concatenate([part[e] for part in parts], axis=1).astype(BF16)
            fbuf[e, :, :, rows] = value.reshape(6, 6, 16, 128)
        return carry

    lax.fori_loop(0, 2, build_f, 0)

    def build_g(k, carry):
        half, pair = lax.div(k, 2), lax.rem(k, 2)
        parts = []
        for n in range(2):
            message = jnp.concatenate([gb[2 * pair + n, 2 * half + m] for m in range(2)], axis=1)
            parts.append(shifted(message.astype(F32).reshape(32, 8, 256), grad_centers, grad_edges))
        rows = pl.ds(pl.multiple_of(16 * pair, 16), 16)
        for e in range(3):
            value = jnp.concatenate([part[e] for part in parts], axis=1).astype(BF16)
            for m in range(2):
                bbuf[2 * half + m, e, :, :, rows] = value[:, :, m * 128 : (m + 1) * 128].reshape(6, 4, 16, 128)
        return carry

    def taps_of(r, tap):
        return jnp.concatenate([wbuf[k, i, r, tap] for i in range(4) for k in range(2)], axis=0)

    def forward(pair):
        acc_f[...] = jnp.zeros_like(acc_f)

        def frame_tap(a, carry):
            windows, taps = [], []
            for b in range(3):
                for e in range(3):
                    windows.append(fbuf[e, b : b + 4, pl.ds(a, 4)].reshape(512, 128))
                    tap = a * 9 + b * 3 + e
                    taps.append(jnp.concatenate([taps_of(2 * pair + k, tap) for k in range(2)], axis=1))
            acc_f[...] += dot(jnp.concatenate(windows, axis=1), jnp.concatenate(taps, axis=0))
            return carry

        lax.fori_loop(0, 3, frame_tap, 0)
        total = acc_f[...].reshape(16, 32, 256)
        for other in range(4):
            psend[pair, other] = total[:, other * 8 : other * 8 + 8].reshape(128, 256).astype(BF16)
        for d in (1, 2, 3):
            src, dst = psend.at[pair, mod4(y + d)], precv.at[pair, d - 1]
            send(src, dst, p_s.at[pair, d - 1], p_r.at[pair, d - 1], y_peers[d - 1])

    def backward():
        acc_b[...] = jnp.zeros_like(acc_b)

        def row_tap(b, carry):
            windows, taps = [], []
            for e in range(3):
                for quad in range(4):
                    windows.append(bbuf[quad, 2 - e, pl.ds(2 - b, 4)].reshape(512, 128))
                    taps.append(jnp.concatenate([taps_of(quad, a * 9 + b * 3 + e) for a in range(3)], axis=0))
            acc_b[...] += lax.dot_general(
                jnp.concatenate(windows, axis=1),
                jnp.concatenate(taps, axis=1),
                (((1,), (1,)), ((), ())),
                preferred_element_type=F32,
            )
            return carry

        lax.fori_loop(0, 3, row_tap, 0)

    sigma = jax.nn.sigmoid(normed)
    slope = sigma * (1.0 + normed * (1.0 - sigma)) * gain
    for k in range(7):
        x_far(k)
    w_layout(2)
    y_far(0)
    y_far(1)
    lax.fori_loop(0, 4, build_g, 0)
    w_core()
    forward(0)
    forward(1)
    backward()
    taps = acc_b[...].reshape(4, 4, 32, 384)
    spread = []
    for u in range(6):
        terms = [taps[:, u - a, :, a * 128 : (a + 1) * 128] for a in range(3) if 0 <= u - a < 4]
        spread.append(sum(terms[1:], terms[0]))
    for other in range(4):
        slots = [part[:, other * 8 : other * 8 + 8] for part in spread]
        bsend[other] = jnp.stack(slots[2:], axis=1).reshape(128, 128).astype(BF16)
        flag = gb[other, 0, 192:208].astype(F32)[6:7]
        dsend[other] = (jnp.stack(slots[:2], axis=1).reshape(64, 128) * flag).astype(BF16)
    for d in (1, 2, 3):
        send(bsend.at[mod4(y + d)], brecv.at[y], b_s.at[d - 1], b_r.at[d - 1], y_peers[d - 1])
    for k in range(4):
        send(dsend.at[k], drecv.at[y], d_s.at[k], d_r.at[y], head_targets[k])
    brecv[y] = bsend[y]
    halves = []
    for pair in range(2):
        total = psend[pair, y].astype(F32)
        for d in (1, 2, 3):
            arrived(precv.at[pair, d - 1], p_r.at[pair, d - 1])
            total = total + precv[pair, d - 1].astype(F32)
        halves.append(total)
    mixed = jnp.concatenate(halves, axis=1)
    out_ref[...] = ((values + swap_frames(mixed)) * live).astype(BF16)
    for copy in started[:-7]:
        copy.wait_send()
    for d in (1, 2, 3):
        arrived(brecv.at[mod4(y - d)], b_r.at[d - 1])
    for k in range(4):
        arrived(drecv.at[k], d_r.at[k])
    own = jnp.concatenate([brecv[k] for k in range(4)], axis=1).astype(F32).reshape(4, 4, 8, 512)
    heads = jnp.concatenate([drecv[k] for k in range(4)], axis=1).astype(F32).reshape(4, 2, 8, 512)
    upstream = swap_lanes(own.reshape(128, 512).astype(BF16), swap_ref).reshape(4, 4, 8, 512)
    tails = swap_lanes(heads.reshape(64, 512).astype(BF16), swap_ref).reshape(4, 2, 8, 512)
    upstream = jnp.concatenate(
        [upstream[:, 0], upstream[:, 1], upstream[:, 2] + tails[:, 0], upstream[:, 3] + tails[:, 1]], axis=0
    ).reshape(128, 512)
    through = upstream * slope
    cubed = scale * scale * scale
    through_mean = jnp.mean(values * through, axis=-1, keepdims=True)
    gradient = masked + scale * through - values * cubed * through_mean
    grad_ref[...] = (gradient * live).astype(BF16)
    for copy in started[-7:]:
        copy.wait_send()


def pin(value):
    return pltpu.with_memory_space_constraint(value, pltpu.HBM)


def per_device(block_input_frames, norm_gain, kernel, output_gradient, group_count, clip_starts):
    shape = block_input_frames.shape
    tables = [jnp.asarray(table(), BF16) for table in (swap_table, column_table, corner_table, edge_table)]
    vmem, smem, hbm = [pl.BlockSpec(memory_space=space) for space in (pltpu.VMEM, pltpu.SMEM, pltpu.HBM)]
    dma = pltpu.SemaphoreType.DMA
    block_out, input_grad = pl.pallas_call(
        body,
        out_shape=[jax.ShapeDtypeStruct((128, 512), BF16)] * 2,
        in_specs=[hbm] * 4 + [smem] * 2 + [hbm] * 4,
        out_specs=[vmem] * 2,
        scratch_shapes=[
            pltpu.VMEM((128, 512), BF16),
            pltpu.VMEM((1, 512), F32),
            pltpu.VMEM((27, 16, 32), BF16),
            pltpu.VMEM((128, 512), BF16),
            *[pltpu.VMEM(table.shape, BF16) for table in tables],
            pltpu.VMEM((4, 16, 112, 128), BF16),
            pltpu.VMEM((2, 4, 4, 27, 16, 128), BF16),
            pltpu.VMEM((128, 512), BF16),
            pltpu.VMEM((128, 512), BF16),
            pltpu.VMEM((2, 96, 512), BF16),
            pltpu.VMEM((2, 96, 512), BF16),
            pltpu.VMEM((2, 64, 128), BF16),
            pltpu.VMEM((2, 64, 128), BF16),
            pltpu.VMEM((4, 384, 128), BF16),
            pltpu.VMEM((4, 384, 128), BF16),
            pltpu.VMEM((4, 4, 256, 128), BF16),
            pltpu.VMEM((3, 6, 6, 32, 128), BF16),
            pltpu.VMEM((4, 3, 6, 4, 32, 128), BF16),
            pltpu.VMEM((512, 256), F32),
            pltpu.VMEM((512, 384), F32),
            pltpu.VMEM((2, 4, 128, 256), BF16),
            pltpu.VMEM((2, 3, 128, 256), BF16),
            pltpu.VMEM((4, 128, 128), BF16),
            pltpu.VMEM((4, 128, 128), BF16),
            pltpu.VMEM((4, 64, 128), BF16),
            pltpu.VMEM((4, 64, 128), BF16),
            dma((8,)),
            dma((8,)), dma((8,)),
            dma((1,)), dma((1,)),
            dma((2, 8)), dma((2, 8)),
            dma((2, 3)), dma((2, 3)),
            dma((2, 3, 2)), dma((2, 3, 2)),
            dma((2, 7)), dma((2, 7)),
            dma((7,)), dma((7,)),
            dma((4,)), dma((4,)),
            dma((2, 3)), dma((2, 3)),
            dma((3,)), dma((3,)),
            dma((4,)), dma((4,)),
        ],
        compiler_params=pltpu.CompilerParams(
            collective_id=0, has_side_effects=True, vmem_limit_bytes=40 * 1024 * 1024
        ),
        cost_estimate=pl.CostEstimate(flops=7_200_000_000, bytes_accessed=20_000_000, transcendentals=200_000),
    )(
        pin(block_input_frames.reshape(128, 512)),
        pin(norm_gain.reshape(1, 512)),
        pin(kernel.reshape(27, 16, 32)),
        pin(output_gradient.reshape(128, 512)),
        group_count,
        clip_starts,
        *[pin(table) for table in tables],
    )
    return block_out.reshape(shape), input_grad.reshape(shape)


def solution(mesh):
    frames = P("group", None, "tile", None, None, None)
    return jax.shard_map(
        per_device,
        mesh=mesh,
        in_specs=(frames, P(), P(None, None, None, "group", "tile"), frames, P("group"), P("group")),
        out_specs=(frames, frames),
        check_vma=False,
    )
```

```python
import numpy as np
import jax
import jax.numpy as jnp
from jax import lax
from jax.experimental import pallas as pl
from jax.experimental.pallas import tpu as pltpu
from jax.sharding import PartitionSpec as P

MESH = pl.DeviceIdType.MESH
EPSILON = 1e-06
F32, BF16 = jnp.float32, jnp.bfloat16


def swap_table():
    table = np.zeros((512, 512), np.float32)
    for a in range(4):
        for b in range(4):
            for o in range(32):
                table[a * 128 + b * 32 + o, b * 128 + a * 32 + o] = 1
    return table.reshape(512, 4, 128).transpose(1, 0, 2)


def column_table():
    table = np.zeros((32, 128), np.float32)
    for it in range(16):
        table[it, it * 8 + 7] = 1
        table[16 + it, it * 8] = 1
    return table


def corner_table():
    table = np.zeros((4, 64, 128), np.float32)
    for k in range(4):
        for corner, (i, j) in enumerate(((3, 7), (3, 0), (0, 7), (0, 0))):
            for t in range(4):
                table[k, 16 * corner + 4 * k + t, (i * 4 + t) * 8 + j] = 1
    return table


def edge_table():
    table = np.zeros((4, 64, 128), np.float32)
    for k in range(4):
        for side in range(2):
            for t in range(4):
                first = 16 * t + 8 * side
                table[k, first, 32 + 16 * side + 4 * k + t] = 1
                table[k, first + 5, 64 + 16 * side + 4 * k + t] = 1
                for i in range(4):
                    table[k, first + 1 + i, 16 * side + i * 4 + t] = 1
    return table


SHARDS = (0, -1, 6, -6, 1, -2, 5, -7, 7, -5, 2, -3, 4, -8, -4, 3)
CHUNKS = ((0, 1, 0), (1, 2, 0), (3, 2, 1), (5, 3, 0), (8, 3, 1), (11, 3, 0), (14, 2, 1))
STRIP_STEPS, COLUMN_STEPS, CORNER_STEPS = (4, -4), (1, -1), (5, 3, -3, -5)


def dot(left, right):
    return jnp.dot(left, right, preferred_element_type=F32)


def swap_lanes(value, swap_ref):
    return dot(value, jnp.concatenate([swap_ref[k] for k in range(4)], axis=1))


def body(
    x_hbm, gain_hbm, w_hbm, g_hbm, count_ref, starts_ref, swap_hbm, column_hbm, corner_hbm, edge_hbm,
    out_ref, grad_ref,
    xv, gainv, wv, gv, swap_ref, column_pick, corner_pick, edge_pick,
    wz, wbuf, tsend, trecv, rows_s, rows_r, corners_s, corners_r, amsg, abuf, gb, fbuf, bbuf,
    acc_f, acc_b, psend, precv, bsend, brecv, dsend, drecv,
    in_s, z_s, z_r, t_s, t_r, h_s, h_r, a_s, a_r, gy_s, gy_r,
    wx_s, wx_r, wf_s, wf_r, wc_s, wc_r, p_s, p_r, b_s, b_r, d_s, d_r,
):
    loads = [
        pltpu.make_async_copy(src, dst, in_s.at[k])
        for k, (src, dst) in enumerate(
            (
                (w_hbm, wv), (g_hbm, gv), (x_hbm, xv), (gain_hbm, gainv), (swap_hbm, swap_ref),
                (column_hbm, column_pick), (corner_hbm, corner_pick), (edge_hbm, edge_pick),
            )
        )
    ]
    for load in loads:
        load.start()

    group = lax.axis_index("group")
    z = lax.axis_index("tile")
    x, y, c = lax.div(group, 8), lax.rem(lax.div(group, 2), 4), lax.rem(group, 2)

    def device(x_at, y_at, c_at, z_at):
        return (x_at * 8 + y_at * 2 + c_at, z_at)

    def mod4(value):
        return lax.rem(value + 4, 4)

    def zmove(step):
        return (group, lax.rem(z + step + 16, 16))

    core = device(x, y, 1 - c, z)
    x_right, x_left = device(mod4(x + 1), y, c, z), device(mod4(x - 1), y, c, z)
    y_peers = [device(x, mod4(y + d), c, z) for d in (1, 2, 3)]
    y_right, y_left = y_peers[0], y_peers[2]
    following, previous = lax.rem(group + 1, 32), lax.rem(group + 31, 32)
    after, before = (following, z), (previous, z)
    head_targets = [(lax.rem(x * 8 + 2 * k + c + 31, 32), z) for k in range(4)]
    head_sources = [device(lax.div(following, 8), k, lax.rem(following, 2), z) for k in range(4)]

    barrier = pltpu.get_barrier_semaphore()
    partners = [core, x_right, x_left, *y_peers, after, before, *head_sources]
    partners += [zmove(step) for step in STRIP_STEPS + COLUMN_STEPS + CORNER_STEPS + (6, -6)]
    for partner in partners:
        pl.semaphore_signal(barrier, inc=1, device_id=partner, device_id_type=MESH)

    started = []

    def remote(src, dst, send_sem, recv_sem, target):
        return pltpu.make_async_remote_copy(
            src_ref=src, dst_ref=dst, send_sem=send_sem, recv_sem=recv_sem, device_id=target, device_id_type=MESH
        )

    def send(src, dst, send_sem, recv_sem, target):
        copy = remote(src, dst, send_sem, recv_sem, target)
        copy.start()
        started.append(copy)

    def arrived(dst, sem):
        remote(dst, dst, sem, sem, core).wait_recv()

    def z_first():
        for k, step in enumerate(SHARDS[1:5]):
            send(wz.at[x, 0], wz.at[x, 1 + k], z_s.at[k], z_r.at[k], zmove(-step))

    def z_first_wait():
        for k in range(4):
            arrived(wz.at[x, 1 + k], z_r.at[k])

    def z_second():
        send(wz.at[x, pl.ds(1, 3)], wz.at[x, pl.ds(5, 3)], z_s.at[4], z_r.at[4], zmove(1))
        send(wz.at[x, pl.ds(2, 3)], wz.at[x, pl.ds(8, 3)], z_s.at[5], z_r.at[5], zmove(-1))

    def z_second_wait():
        arrived(wz.at[x, pl.ds(5, 3)], z_r.at[4])
        arrived(wz.at[x, pl.ds(8, 3)], z_r.at[5])

    def z_third():
        send(wz.at[x, pl.ds(5, 3)], wz.at[x, pl.ds(11, 3)], z_s.at[6], z_r.at[6], zmove(1))
        send(wz.at[x, pl.ds(9, 2)], wz.at[x, pl.ds(14, 2)], z_s.at[7], z_r.at[7], zmove(-1))

    def z_third_wait():
        arrived(wz.at[x, pl.ds(11, 3)], z_r.at[6])
        arrived(wz.at[x, pl.ds(14, 2)], z_r.at[7])

    def x_block(step, k):
        return wz.at[mod4(x + step), pl.ds(CHUNKS[k][0], CHUNKS[k][1])]

    def x_send(k, side):
        block = x_block(0, k)
        send(block, block, wx_s.at[side, k], wx_r.at[side, k], x_left if side else x_right)

    def x_arrived(k, side):
        arrived(x_block(1 if side else -1, k), wx_r.at[side, k])

    def x_pass(k):
        side = CHUNKS[k][2]
        x_arrived(k, side)
        block = x_block(1 if side else -1, k)
        send(block, block, wf_s.at[k], wf_r.at[k], x_left if side else x_right)

    def x_far(k):
        arrived(x_block(2, k), wf_r.at[k])

    places = []
    for shard in range(16):
        away = lax.rem(shard - z + 24, 16) - 8
        place = jnp.int32(0)
        for slot in range(1, 16):
            place = jnp.where(away == SHARDS[slot], slot, place)
        places.append(place)

    def w_layout(step):
        at = mod4(x + step)
        rows = []
        for quad in range(4):
            rows.append(jnp.concatenate([wz[at, places[quad * 4 + j]] for j in range(4)], axis=1))
        full = swap_lanes(jnp.concatenate(rows, axis=0), swap_ref).astype(BF16)
        for quad in range(4):
            for tap in range(27):
                row, lanes = quad * 112 + (tap // 4) * 16, (tap % 4) * 128
                wbuf[c, at, quad, tap] = full[row : row + 16, lanes : lanes + 128]
        whole = wbuf.at[c, at]
        send(whole, whole, wc_s.at[step + 1], wc_r.at[step + 1], core)

    def w_core():
        for step in (0, -1, 1, 2):
            arrived(wbuf.at[1 - c, mod4(x + step)], wc_r.at[step + 1])

    def y_block(owner, half, part):
        return gb.at[owner, pl.ds(2 * half, 2), pl.ds(128 * part, 128)]

    def y_start(part):
        for half in range(2):
            block = y_block(y, half, part)
            send(block, block, gy_s.at[part, 0, half], gy_r.at[part, 0, half], y_right)
            send(block, block, gy_s.at[part, 1, half], gy_r.at[part, 1, half], y_left)

    def y_relay(part):
        for side, step, target in ((0, -1, y_right), (1, 1, y_left)):
            for half in (side, 1 - side):
                block = y_block(mod4(y + step), half, part)
                arrived(block, gy_r.at[part, side, half])
                if half == side:
                    send(block, block, gy_s.at[part, 2, half], gy_r.at[part, 2, half], target)

    def y_far(part):
        for half in range(2):
            arrived(y_block(mod4(y + 2), half, part), gy_r.at[part, 2, half])

    def strips_start(field, tile):
        rows_s[field, 0:32] = tile[96:128]
        rows_s[field, 32:64] = tile[0:32]
        for k, step in enumerate(STRIP_STEPS):
            block = pl.ds(32 * k, 32)
            send(rows_s.at[field, block], rows_r.at[field, block], h_s.at[field, k], h_r.at[field, k], zmove(step))

    def columns_start(field, tile):
        rows_s[field, 64:96] = dot(column_pick[...], tile).astype(BF16)
        for k, step in enumerate(COLUMN_STEPS):
            block = pl.ds(64 + 16 * k, 16)
            send(rows_s.at[field, block], rows_r.at[field, block], h_s.at[field, 2 + k], h_r.at[field, 2 + k], zmove(step))
        corners = [dot(corner_pick[k], tile[:, k * 128 : (k + 1) * 128]) for k in range(4)]
        corners_s[field] = (corners[0] + corners[1] + corners[2] + corners[3]).astype(BF16)
        for k, step in enumerate(CORNER_STEPS):
            block = pl.ds(16 * k, 16)
            send(corners_s.at[field, block], corners_r.at[field, block], h_s.at[field, 4 + k], h_r.at[field, 4 + k], zmove(step))

    tile_row, tile_column = lax.div(z, 4), lax.rem(z, 4)

    def unless(hit):
        return jnp.where(hit, 0.0, 1.0).astype(F32)

    at_top, at_bottom = unless(tile_row == 0), unless(tile_row == 3)
    at_left, at_right = unless(tile_column == 0), unless(tile_column == 3)

    def halo_finish(field):
        for k in range(2):
            arrived(rows_r.at[field, pl.ds(32 * k, 32)], h_r.at[field, k])
        for k in range(2):
            arrived(rows_r.at[field, pl.ds(64 + 16 * k, 16)], h_r.at[field, 2 + k])
        for k in range(4):
            arrived(corners_r.at[field, pl.ds(16 * k, 16)], h_r.at[field, 4 + k])
        above = rows_r[field, 0:32].astype(F32) * at_top
        below = rows_r[field, 32:64].astype(F32) * at_bottom
        row_at = lax.broadcasted_iota(jnp.int32, (64, 128), 0)
        keep = jnp.where((row_at & 8) == 0, at_left, at_right)
        keep = keep * jnp.where((row_at & 7) == 0, at_top, 1.0) * jnp.where((row_at & 7) == 5, at_bottom, 1.0)
        flag = jnp.where(row_at == 6, source, 0.0)
        edges = []
        for k in range(4):
            picks = jnp.concatenate([rows_r[field, 64:96, k * 128 : (k + 1) * 128], corners_r[field]], axis=0)
            edges.append(dot(edge_pick[k, :, 0:96], picks) * keep + flag)
        return jnp.concatenate([above, below, jnp.concatenate(edges, axis=1)], axis=0).astype(BF16)

    loads[0].wait()
    packed = jnp.zeros((112, 128), F32)
    for k in range(4):
        taps = [wv[4 * row + k] if 4 * row + k < 27 else jnp.zeros((16, 32), BF16) for row in range(7)]
        lane_at = lax.broadcasted_iota(jnp.int32, (32, 128), 1) - lax.broadcasted_iota(jnp.int32, (32, 128), 0)
        packed = packed + dot(jnp.concatenate(taps, axis=0), jnp.where(lane_at == 32 * k, 1.0, 0.0).astype(BF16))
    wz[x, 0] = packed.astype(BF16)

    live = jnp.where(count_ref[0] > 0, 1.0, 0.0).astype(F32)
    fresh = jnp.where(starts_ref[0] == 0, 1.0, 0.0).astype(F32)
    source = live * fresh * jnp.where(group > 0, 1.0, 0.0).astype(F32)

    def swap_frames(value):
        value = value.reshape(4, 4, 8, value.shape[1])
        return jnp.concatenate([value[:, k] for k in range(4)], axis=0).reshape(128, value.shape[3])

    loads[1].wait()
    masked = gv[...].astype(F32) * live
    grad_tile = swap_frames(masked).astype(BF16)
    for k in range(4):
        gb[y, k, 0:128] = grad_tile[:, k * 128 : (k + 1) * 128]

    pl.semaphore_wait(barrier, len(partners))
    z_first()
    x_send(0, 0)
    x_send(0, 1)
    y_start(0)

    loads[2].wait()
    loads[3].wait()
    loads[4].wait()
    gain = gainv[...]
    values = xv[...].astype(F32)
    scale = lax.rsqrt(jnp.mean(values * values, axis=-1, keepdims=True) + EPSILON)
    normed = values * scale * gain
    activated = (normed * jax.nn.sigmoid(normed)).astype(BF16)
    swapped = swap_lanes(activated, swap_ref)
    tsend[0:64] = swapped[64:128].astype(BF16)
    act_tile = swap_frames(swapped).astype(BF16)

    def a_rows(part):
        return pl.ds(0, 128) if part == 0 else pl.ds(128, 256)

    def a_start(part, value):
        first = 0 if part == 0 else 128
        for k in range(4):
            amsg[k, first : first + value.shape[0]] = value[:, k * 128 : (k + 1) * 128]
        for d in (1, 2, 3):
            src, dst = amsg.at[mod4(y + d), a_rows(part)], abuf.at[y, a_rows(part)]
            send(src, dst, a_s.at[part, d - 1], a_r.at[part, d - 1], y_peers[d - 1])
        abuf[y, first : first + value.shape[0]] = amsg[y, first : first + value.shape[0]]

    def a_wait(part):
        for d in (1, 2, 3):
            arrived(abuf.at[mod4(y - d), a_rows(part)], a_r.at[part, d - 1])

    a_start(0, act_tile)
    for load in loads[5:]:
        load.wait()
    strips_start(0, act_tile)
    columns_start(0, act_tile)
    z_first_wait()
    z_second()
    for k, side in ((1, 0), (2, 1), (2, 0), (1, 1)):
        x_send(k, side)
    strips_start(1, grad_tile)
    columns_start(1, grad_tile)
    x_pass(0)
    y_relay(0)
    halo = halo_finish(0)
    tsend[64:80] = halo[16:32]
    tsend[80:96] = halo[48:64]
    tsend[96:128] = halo[96:128]
    send(tsend, trecv, t_s.at[0], t_r.at[0], after)
    z_second_wait()
    z_third()
    for k, side in ((3, 0), (4, 1), (4, 0), (3, 1)):
        x_send(k, side)
    x_pass(1)
    x_pass(2)
    grad_halo = halo_finish(1)
    for k in range(4):
        gb[y, k, 128:256] = grad_halo[:, k * 128 : (k + 1) * 128]
    y_start(1)
    z_third_wait()
    for k, side in ((5, 0), (6, 1), (6, 0), (5, 1)):
        x_send(k, side)
    x_pass(3)
    x_pass(4)
    w_layout(0)
    arrived(trecv, t_r.at[0])
    a_start(1, jnp.concatenate([halo, (trecv[...].astype(F32) * source).astype(BF16)], axis=0))
    y_relay(1)
    x_pass(5)
    x_pass(6)
    for k in range(7):
        x_arrived(k, 1 - CHUNKS[k][2])
    w_layout(-1)
    w_layout(1)

    def shifted(slabs, centers, edges):
        center = jnp.concatenate([slabs[k : k + 1] for k in centers], axis=0)
        sides = []
        for side in range(2):
            rows = [jnp.broadcast_to(slabs[k + side, i : i + 1], slabs.shape[1:])[None] for k, i in edges]
            sides.append(jnp.concatenate(rows, axis=0))
        at = lax.broadcasted_iota(jnp.int32, center.shape, 1)
        from_left = jnp.where(at == 0, sides[0], pltpu.roll(center, 1, 1))
        from_right = jnp.where(at == 7, sides[1], pltpu.roll(center, 7, 1))
        return from_left, center, from_right

    def own_slab(i, t):
        return 16 + t if i == 0 else 20 + t if i == 5 else (i - 1) * 4 + t

    def carried_slab(i, t):
        return 40 + t if i == 0 else 42 + t if i == 5 else 32 + t * 4 + i - 1

    grad_centers = [own_slab(i, t) for i in range(6) for t in range(4)]
    grad_edges = [(24 + 2 * t, i) for i in range(6) for t in range(4)]
    act_centers = [carried_slab(i, t) if t < 2 else own_slab(i, t - 2) for i in range(6) for t in range(6)]
    act_edges = [(44 + 2 * t, i) if t < 2 else (24 + 2 * (t - 2), i) for i in range(6) for t in range(6)]

    a_wait(0)
    a_wait(1)

    def build_f(pair, carry):
        parts = []
        for k in range(2):
            slabs = abuf[2 * pair + k].astype(F32).reshape(48, 8, 128)
            parts.append(shifted(slabs, act_centers, act_edges))
        rows = pl.ds(pl.multiple_of(16 * pair, 16), 16)
        for e in range(3):
            value = jnp.concatenate([part[e] for part in parts], axis=1).astype(BF16)
            fbuf[e, :, :, rows] = value.reshape(6, 6, 16, 128)
        return carry

    lax.fori_loop(0, 2, build_f, 0)

    def build_g(k, carry):
        half, pair = lax.div(k, 2), lax.rem(k, 2)
        parts = []
        for n in range(2):
            message = jnp.concatenate([gb[2 * pair + n, 2 * half + m] for m in range(2)], axis=1)
            parts.append(shifted(message.astype(F32).reshape(32, 8, 256), grad_centers, grad_edges))
        rows = pl.ds(pl.multiple_of(16 * pair, 16), 16)
        for e in range(3):
            value = jnp.concatenate([part[e] for part in parts], axis=1).astype(BF16)
            for m in range(2):
                bbuf[2 * half + m, e, :, :, rows] = value[:, :, m * 128 : (m + 1) * 128].reshape(6, 4, 16, 128)
        return carry

    def taps_of(r, tap):
        return jnp.concatenate([wbuf[k, i, r, tap] for i in range(4) for k in range(2)], axis=0)

    def forward(pair):
        acc_f[...] = jnp.zeros_like(acc_f)

        def frame_tap(a, carry):
            windows, taps = [], []
            for b in range(3):
                for e in range(3):
                    windows.append(fbuf[e, b : b + 4, pl.ds(a, 4)].reshape(512, 128))
                    tap = a * 9 + b * 3 + e
                    taps.append(jnp.concatenate([taps_of(2 * pair + k, tap) for k in range(2)], axis=1))
            acc_f[...] += dot(jnp.concatenate(windows, axis=1), jnp.concatenate(taps, axis=0))
            return carry

        lax.fori_loop(0, 3, frame_tap, 0)
        total = acc_f[...].reshape(16, 32, 256)
        for other in range(4):
            psend[pair, other] = total[:, other * 8 : other * 8 + 8].reshape(128, 256).astype(BF16)
        for d in (1, 2, 3):
            src, dst = psend.at[pair, mod4(y + d)], precv.at[pair, d - 1]
            send(src, dst, p_s.at[pair, d - 1], p_r.at[pair, d - 1], y_peers[d - 1])

    def backward():
        acc_b[...] = jnp.zeros_like(acc_b)

        def row_tap(b, carry):
            windows, taps = [], []
            for e in range(3):
                for quad in range(4):
                    windows.append(bbuf[quad, 2 - e, pl.ds(2 - b, 4)].reshape(512, 128))
                    taps.append(jnp.concatenate([taps_of(quad, a * 9 + b * 3 + e) for a in range(3)], axis=0))
            acc_b[...] += lax.dot_general(
                jnp.concatenate(windows, axis=1),
                jnp.concatenate(taps, axis=1),
                (((1,), (1,)), ((), ())),
                preferred_element_type=F32,
            )
            return carry

        lax.fori_loop(0, 3, row_tap, 0)

    sigma = jax.nn.sigmoid(normed)
    slope = sigma * (1.0 + normed * (1.0 - sigma)) * gain
    for k in range(7):
        x_far(k)
    w_layout(2)
    y_far(0)
    y_far(1)
    lax.fori_loop(0, 4, build_g, 0)
    w_core()
    forward(0)
    forward(1)
    backward()
    taps = acc_b[...].reshape(4, 4, 32, 384)
    spread = []
    for u in range(6):
        terms = [taps[:, u - a, :, a * 128 : (a + 1) * 128] for a in range(3) if 0 <= u - a < 4]
        spread.append(sum(terms[1:], terms[0]))
    for other in range(4):
        slots = [part[:, other * 8 : other * 8 + 8] for part in spread]
        bsend[other] = jnp.stack(slots[2:], axis=1).reshape(128, 128).astype(BF16)
        flag = gb[other, 0, 192:208].astype(F32)[6:7]
        dsend[other] = (jnp.stack(slots[:2], axis=1).reshape(64, 128) * flag).astype(BF16)
    for d in (1, 2, 3):
        send(bsend.at[mod4(y + d)], brecv.at[y], b_s.at[d - 1], b_r.at[d - 1], y_peers[d - 1])
    for k in range(4):
        send(dsend.at[k], drecv.at[y], d_s.at[k], d_r.at[y], head_targets[k])
    brecv[y] = bsend[y]
    halves = []
    for pair in range(2):
        total = psend[pair, y].astype(F32)
        for d in (1, 2, 3):
            arrived(precv.at[pair, d - 1], p_r.at[pair, d - 1])
            total = total + precv[pair, d - 1].astype(F32)
        halves.append(total)
    mixed = jnp.concatenate(halves, axis=1)
    out_ref[...] = ((values + swap_frames(mixed)) * live).astype(BF16)
    for copy in started[:-7]:
        copy.wait_send()
    for d in (1, 2, 3):
        arrived(brecv.at[mod4(y - d)], b_r.at[d - 1])
    for k in range(4):
        arrived(drecv.at[k], d_r.at[k])
    own = jnp.concatenate([brecv[k] for k in range(4)], axis=1).astype(F32).reshape(4, 4, 8, 512)
    heads = jnp.concatenate([drecv[k] for k in range(4)], axis=1).astype(F32).reshape(4, 2, 8, 512)
    upstream = swap_lanes(own.reshape(128, 512).astype(BF16), swap_ref).reshape(4, 4, 8, 512)
    tails = swap_lanes(heads.reshape(64, 512).astype(BF16), swap_ref).reshape(4, 2, 8, 512)
    upstream = jnp.concatenate(
        [upstream[:, 0], upstream[:, 1], upstream[:, 2] + tails[:, 0], upstream[:, 3] + tails[:, 1]], axis=0
    ).reshape(128, 512)
    through = upstream * slope
    cubed = scale * scale * scale
    through_mean = jnp.mean(values * through, axis=-1, keepdims=True)
    gradient = masked + scale * through - values * cubed * through_mean
    grad_ref[...] = (gradient * live).astype(BF16)
    for copy in started[-7:]:
        copy.wait_send()


def pin(value):
    return pltpu.with_memory_space_constraint(value, pltpu.HBM)


def per_device(block_input_frames, norm_gain, kernel, output_gradient, group_count, clip_starts):
    shape = block_input_frames.shape
    tables = [jnp.asarray(table(), BF16) for table in (swap_table, column_table, corner_table, edge_table)]
    vmem, smem, hbm = [pl.BlockSpec(memory_space=space) for space in (pltpu.VMEM, pltpu.SMEM, pltpu.HBM)]
    dma = pltpu.SemaphoreType.DMA
    block_out, input_grad = pl.pallas_call(
        body,
        out_shape=[jax.ShapeDtypeStruct((128, 512), BF16)] * 2,
        in_specs=[hbm] * 4 + [smem] * 2 + [hbm] * 4,
        out_specs=[vmem] * 2,
        scratch_shapes=[
            pltpu.VMEM((128, 512), BF16),
            pltpu.VMEM((1, 512), F32),
            pltpu.VMEM((27, 16, 32), BF16),
            pltpu.VMEM((128, 512), BF16),
            *[pltpu.VMEM(table.shape, BF16) for table in tables],
            pltpu.VMEM((4, 16, 112, 128), BF16),
            pltpu.VMEM((2, 4, 4, 27, 16, 128), BF16),
            pltpu.VMEM((128, 512), BF16),
            pltpu.VMEM((128, 512), BF16),
            pltpu.VMEM((2, 96, 512), BF16),
            pltpu.VMEM((2, 96, 512), BF16),
            pltpu.VMEM((2, 64, 128), BF16),
            pltpu.VMEM((2, 64, 128), BF16),
            pltpu.VMEM((4, 384, 128), BF16),
            pltpu.VMEM((4, 384, 128), BF16),
            pltpu.VMEM((4, 4, 256, 128), BF16),
            pltpu.VMEM((3, 6, 6, 32, 128), BF16),
            pltpu.VMEM((4, 3, 6, 4, 32, 128), BF16),
            pltpu.VMEM((512, 256), F32),
            pltpu.VMEM((512, 384), F32),
            pltpu.VMEM((2, 4, 128, 256), BF16),
            pltpu.VMEM((2, 3, 128, 256), BF16),
            pltpu.VMEM((4, 128, 128), BF16),
            pltpu.VMEM((4, 128, 128), BF16),
            pltpu.VMEM((4, 64, 128), BF16),
            pltpu.VMEM((4, 64, 128), BF16),
            dma((8,)),
            dma((8,)), dma((8,)),
            dma((1,)), dma((1,)),
            dma((2, 8)), dma((2, 8)),
            dma((2, 3)), dma((2, 3)),
            dma((2, 3, 2)), dma((2, 3, 2)),
            dma((2, 7)), dma((2, 7)),
            dma((7,)), dma((7,)),
            dma((4,)), dma((4,)),
            dma((2, 3)), dma((2, 3)),
            dma((3,)), dma((3,)),
            dma((4,)), dma((4,)),
        ],
        compiler_params=pltpu.CompilerParams(
            collective_id=0, has_side_effects=True, vmem_limit_bytes=40 * 1024 * 1024
        ),
        cost_estimate=pl.CostEstimate(flops=7_200_000_000, bytes_accessed=20_000_000, transcendentals=200_000),
    )(
        pin(block_input_frames.reshape(128, 512)),
        pin(norm_gain.reshape(1, 512)),
        pin(kernel.reshape(27, 16, 32)),
        pin(output_gradient.reshape(128, 512)),
        group_count,
        clip_starts,
        *[pin(table) for table in tables],
    )
    return block_out.reshape(shape), input_grad.reshape(shape)


def solution(mesh):
    frames = P("group", None, "tile", None, None, None)
    return jax.shard_map(
        per_device,
        mesh=mesh,
        in_specs=(frames, P(), P(None, None, None, "group", "tile"), frames, P("group"), P("group")),
        out_specs=(frames, frames),
        check_vma=False,
    )
```
